32 devices in a mesh: dp: 8 (over z, x), seq: 4 (over y, core).
Axes of the slice: x: 2, y: 2, z: 4, core: 2. Of those that a mesh axis runs over, the one named last changes fastest.
Arguments:
- tokens: bfloat16 [16, 2048, 1088], P('dp', 'seq'), may hold values from -6 to 6
- qkv_weight: bfloat16 [1088, 3264], P('dp'), may hold values from -0.1875 to 0.1875
- out_weight: bfloat16 [1088, 1088], P('dp'), may hold values from -0.75 to 0.75
- up_weight: bfloat16 [1088, 4352], P('dp'), may hold values from -0.1875 to 0.1875
- down_weight: bfloat16 [4352, 1088], P('dp'), may hold values from -0.09375 to 0.09375
- norm_gain: bfloat16 [2, 1088], P(None, 'dp'), may hold values from 0.5 to 1.5
- norm_shift: bfloat16 [2, 1088], P(None, 'dp'), may hold values from -4 to 4
- bias_rows: bfloat16 [4, 1088], P(None, 'dp'), may hold values from -6 to 6
- bias_hidden: bfloat16 [4352], P('dp'), may hold values from -6 to 6
- doc_lengths: int32 [16, 6], P('dp'), may hold values from 32 to 1888, as said below
- cotangent: bfloat16 [16, 2048, 1088], P('dp', 'seq'), may hold values from -6 to 6
Outputs:
- layer_out: bfloat16 [16, 2048, 1088], P('dp', 'seq')
- grad_tokens: float32 [16, 2048, 1088], P('dp', 'seq')
- grad_qkv: float32 [1088, 3264], P('dp')
- grad_out_weight: float32 [1088, 1088], P('dp')
- grad_up: float32 [1088, 4352], P('dp')
- grad_down: float32 [4352, 1088], P('dp')
- grad_gain: float32 [2, 1088], P(None, 'dp')
- grad_shift: float32 [2, 1088], P(None, 'dp')
- grad_bias_rows: float32 [4, 1088], P(None, 'dp')
- grad_bias_hidden: float32 [4352], P('dp')
The draws below stay inside these ranges and needn't reach their ends.
Inputs may be any that keep to these rules, and one draw needn't show every extreme that they name: `doc_lengths`: each row lists the lengths of the 6 documents packed into one sequence, in order; they sum to 2048.
All inputs are finite; a program needn't handle non-finite values.
Results may differ from the reference program's by a relative error of at most 0.015.
Values may be sent and summed in bfloat16 or wider, within the bound.
No kernel may reach another device: no remote copies, remote signals or barrier semaphores. Data moves between devices by JAX's collectives and lax.ppermute only.
A program may use at most 384 MiB of HBM per device.

```python
import jax
import jax.numpy as jnp
from jax import lax

D = 1088
H = 17
HD = 64
FF = 4352
LEN = 2048
DOCS = 6
MICRO = 2
SEQS = 16


def draw_doc_lengths(key, part):
    key = jax.random.fold_in(key, 11)
    key_short, key_place, key_pick, key_packed = jax.random.split(key, 4)
    shorts = jax.random.randint(key_short, (SEQS, DOCS), LEN // 64, LEN // 24 + 1, dtype=jnp.int32)
    first_row = (jnp.arange(SEQS, dtype=jnp.int32) == 0)[:, None]
    shorts = jnp.where(first_row, LEN // 64, shorts)
    long_place = jax.random.randint(key_place, (SEQS, 1), 0, DOCS, dtype=jnp.int32)
    is_long = jnp.arange(DOCS, dtype=jnp.int32)[None, :] == long_place
    shorts = jnp.where(is_long, 0, shorts)
    long_len = LEN - jnp.sum(shorts, axis=1, keepdims=True)
    spanning_rows = jnp.where(is_long, long_len, shorts).astype(jnp.int32)
    least_len = max(1, LEN // 34)
    most_len = LEN * 25 // 64
    remaining = jnp.full((SEQS,), LEN, dtype=jnp.int32)
    doc_keys = jax.random.split(key_packed, DOCS)
    columns = []
    for doc in range(DOCS - 1):
        later = DOCS - 1 - doc
        lower_bound = jnp.maximum(least_len, remaining - later * most_len)
        upper_bound = jnp.minimum(most_len, remaining - later * least_len)
        length_now = jax.random.randint(doc_keys[doc], (SEQS,), lower_bound, upper_bound + 1, dtype=jnp.int32)
        columns.append(length_now)
        remaining = remaining - length_now
    columns.append(remaining)
    packed_rows = jnp.stack(columns, axis=1).astype(jnp.int32)
    groups = SEQS // MICRO
    picked = jax.random.randint(key_pick, (groups,), 0, MICRO, dtype=jnp.int32)
    picked = jnp.where(jnp.arange(groups, dtype=jnp.int32) == 0, 0, picked)
    row_ids = jnp.arange(SEQS, dtype=jnp.int32)
    spanning = row_ids % MICRO == picked[row_ids // MICRO]
    return jnp.where(spanning[:, None], spanning_rows, packed_rows).astype(jnp.int32)


def shard_levels(own_key, extent, cuts, smallest, largest):
    def one(dim, shards_of):
        steps = jax.random.uniform(jax.random.fold_in(jax.random.fold_in(own_key, 6), dim), (shards_of,), jnp.float32, smallest / len(cuts), largest / len(cuts))
        return jnp.repeat(jnp.exp(steps), extent[dim] // shards_of).reshape((-1,) + (1,) * (len(extent) - dim - 1))

    level = one(*cuts[0])
    for cut in cuts[1:]:
        level = level * one(*cut)
    return level


def gaussian(own_key, dims, scale, limit, pieces=(), kind=jnp.bfloat16):
    array = jax.random.normal(own_key, dims, jnp.float32) * scale
    if len(pieces) > 0:
        array = shard_levels(own_key, dims, pieces, -0.22, 0.18) * array
    return jnp.clip(array, min=-limit, max=limit).astype(kind)


def setup_inputs(seed: int = 0) -> dict:
    seeds = jax.random.split(jax.random.key(seed), 12)
    return {
        "tokens": gaussian(seeds[0], (SEQS, LEN, D), 1.0, 6.0, ((0, 8), (1, 4))),
        "qkv_weight": gaussian(seeds[1], (D, 3 * D), D ** -0.5, 0.1875, ((0, 8),)),
        "out_weight": gaussian(seeds[2], (D, D), (D // 16) ** -0.5, 0.75, ((0, 8),)),
        "up_weight": gaussian(seeds[3], (D, FF), D ** -0.5, 0.1875, ((0, 8),)),
        "down_weight": gaussian(seeds[4], (FF, D), FF ** -0.5, 0.09375, ((0, 8),)),
        "norm_gain": jnp.clip(1.0 + 0.1 * jax.random.normal(seeds[5], (2, D), jnp.float32), 0.5, 1.5).astype(jnp.bfloat16),
        "norm_shift": gaussian(seeds[6], (2, D), 0.3, 4.0, ((1, 8),)),
        "bias_rows": gaussian(seeds[7], (4, D), 0.5, 6.0, ((1, 8),)),
        "bias_hidden": gaussian(seeds[8], (FF,), 0.5, 6.0, ((0, 8),)),
        "doc_lengths": draw_doc_lengths(jax.random.fold_in(seeds[11], 71), 0),
        "cotangent": gaussian(seeds[10], (SEQS, LEN, D), 1.0, 6.0, ((0, 8), (1, 4))),
    }


@jax.custom_vjp
def low(v):
    return lax.optimization_barrier(v.astype(jnp.bfloat16)).astype(jnp.float32)

@jax.custom_vjp
def low_back(v):
    return v

def low_keep(v):
    return (low(v), None)

def low_pass(kept, grad):
    return (grad,)

def back_keep(v):
    return (v, None)

def back_low(kept, grad):
    return (low(grad),)
low.defvjp(low_keep, low_pass)
low_back.defvjp(back_keep, back_low)
norm_eps = 1e-05
masked_score = -1e+30

def matmul_high(left, right):
    return jnp.dot(left, right, precision=lax.Precision.HIGHEST)

def layer_norm(values_in, gain_row, shift_row):
    centre = values_in - lax.optimization_barrier(jnp.mean(values_in, axis=-1, keepdims=True))
    spread = lax.optimization_barrier(jnp.mean(centre * centre, axis=-1, keepdims=True))
    return centre * lax.rsqrt(spread + norm_eps) * gain_row + shift_row

def segment_ids(doc_lengths, positions):
    bounds = jnp.cumsum(doc_lengths).astype(jnp.int32)[:-1]
    return lax.optimization_barrier(jnp.sum((positions[:, None] >= bounds[None, :]).astype(jnp.int32), axis=1))

def one_sequence(params, seq_tokens, doc_lengths):
    qkv_weight, out_weight, up_weight, down_weight, norm_gain, norm_shift, bias_rows, bias_hidden = params
    positions = jnp.arange(LEN, dtype=jnp.int32)
    seg_ids = segment_ids(doc_lengths, positions)
    allowed = (positions[:, None] >= positions[None, :]) & (seg_ids[:, None] == seg_ids[None, :])
    normed = low(layer_norm(seq_tokens, norm_gain[0], norm_shift[0]))
    joined = matmul_high(normed, qkv_weight)
    query_rows = low(low_back(joined[:, :D] + bias_rows[0])).reshape(LEN, H, HD)
    key_rows = low(low_back(joined[:, D:2 * D])).reshape(LEN, H, HD)
    value_rows = low(low_back(joined[:, 2 * D:] + bias_rows[1])).reshape(LEN, H, HD)
    scores = jnp.einsum('qhd,khd->hqk', query_rows, key_rows, precision=lax.Precision.HIGHEST) * HD ** (-0.5)
    scores = jnp.where(allowed[None], low_back(scores), masked_score)
    row_peak = lax.optimization_barrier(jnp.max(scores, axis=-1, keepdims=True))
    weights_exp = jnp.exp(scores - row_peak)
    prob_rows = low(weights_exp / lax.optimization_barrier(jnp.sum(weights_exp, axis=-1, keepdims=True)))
    mixed_heads = jnp.einsum('hqk,khd->qhd', prob_rows, value_rows, precision=lax.Precision.HIGHEST).reshape(LEN, D)
    mixed_heads = low(low_back(mixed_heads))
    attn_branch = low_back(matmul_high(mixed_heads, out_weight) + bias_rows[2])
    residual = seq_tokens + attn_branch
    normed_two = low(layer_norm(residual, norm_gain[1], norm_shift[1]))
    up_proj = low_back(matmul_high(normed_two, up_weight) + bias_hidden)
    active = low(jax.nn.gelu(up_proj, approximate=True))
    branch = low_back(matmul_high(active, down_weight) + bias_rows[3])
    return residual + branch

def reference(tokens, qkv_weight, out_weight, up_weight, down_weight, norm_gain, norm_shift, bias_rows, bias_hidden, doc_lengths, cotangent):
    params = (qkv_weight.astype(jnp.float32), out_weight.astype(jnp.float32), up_weight.astype(jnp.float32), down_weight.astype(jnp.float32), norm_gain.astype(jnp.float32), norm_shift.astype(jnp.float32), bias_rows.astype(jnp.float32), bias_hidden.astype(jnp.float32))
    x_float = tokens.astype(jnp.float32)

    def forward(params_in, tokens_in):

        def per_sequence(seq_entry):
            return jax.checkpoint(one_sequence)(params_in, seq_entry[0], seq_entry[1])
        return lax.map(per_sequence, (tokens_in, doc_lengths))
    outputs, pullback = jax.vjp(forward, params, x_float)
    param_grads, grad_tokens = pullback(cotangent.astype(jnp.float32))
    return (outputs.astype(jnp.bfloat16), grad_tokens, param_grads[0], param_grads[1], param_grads[2], param_grads[3], param_grads[4], param_grads[5], param_grads[6], param_grads[7])
```

```python
import functools

import jax
import jax.numpy as jnp
from jax import lax
from jax.experimental import pallas as pl
from jax.experimental.pallas import tpu as pltpu
from jax.sharding import PartitionSpec as P

D = 1088
H = 17
HD = 64
FF = 4352

norm_eps = 1e-05
masked_score = -1e30
score_scale = HD ** (-0.5)

TQ = 512
TK = 512
VMEM_BYTES = 56 * 1024 * 1024

f32 = jnp.float32
bf16 = jnp.bfloat16


def dot_tn(left, right):
    return lax.dot_general(left, right, (((0,), (0,)), ((), ())), preferred_element_type=f32)


def dot_nn(left, right):
    return lax.dot_general(left, right, (((1,), (0,)), ((), ())), preferred_element_type=f32)


def dot_nt(left, right):
    return lax.dot_general(left, right, (((1,), (1,)), ((), ())), preferred_element_type=f32)


def norm_stats(rows):
    centre = rows - jnp.mean(rows, axis=0, keepdims=True)
    spread = jnp.mean(centre * centre, axis=0, keepdims=True)
    inverse = lax.rsqrt(spread + norm_eps)
    return centre * inverse, inverse


def norm_back(grad, unit, inverse, gain):
    scaled = grad * gain
    mean_one = jnp.mean(scaled, axis=0, keepdims=True)
    mean_two = jnp.mean(scaled * unit, axis=0, keepdims=True)
    return inverse * (scaled - mean_one - unit * mean_two)


def place_blocks(info_ref, store):
    for which in range(4):
        store(which // 2, which % 2, info_ref[which])


def allowed_mask(key_first, query_first, start_row):
    shape = (TK, TQ)
    key_pos = key_first + lax.broadcasted_iota(jnp.int32, shape, 0)
    query_pos = query_first + lax.broadcasted_iota(jnp.int32, shape, 1)
    return (key_pos <= query_pos) & (key_pos >= start_row)


def attend_kernel(
    info_ref, query_ref, key_ref, value_ref, key_sib_ref, value_sib_ref, start_ref,
    mixed_ref, log_ref, key_s, value_s,
):
    half = query_ref.shape[1] // 2
    ones_rows = jnp.ones((16, half), bf16)

    def store(sibling, part, block):
        key_from, value_from = (key_sib_ref, value_sib_ref) if sibling else (key_ref, value_ref)
        lanes = slice(part * half, (part + 1) * half)
        key_s[block] = key_from[:, lanes].astype(f32).T.astype(bf16)
        value_s[block] = jnp.concatenate([value_from[:, lanes], ones_rows], axis=0)

    place_blocks(info_ref, store)
    for part in range(2):
        lanes = slice(part * half, (part + 1) * half)
        query = query_ref[:, lanes] * jnp.asarray(score_scale, bf16)
        start_row = start_ref[:, lanes]
        own_block = info_ref[part]
        first = info_ref[4 + part]
        clear = info_ref[6 + part]

        def step(block, state, masked, query=query, start_row=start_row, own_block=own_block):
            peak, total = state
            scores = dot_nn(key_s[block], query)
            if masked:
                scores = jnp.where(
                    allowed_mask(block * TK, own_block * TQ, start_row), scores, masked_score
                )
            new_peak = jnp.maximum(peak, jnp.max(scores, axis=0, keepdims=True))
            weights = jnp.exp(scores - new_peak).astype(bf16)
            total = total * jnp.exp(peak - new_peak) + dot_nn(value_s[block], weights)
            return new_peak, total

        state = (
            jnp.full((1, half), masked_score, f32),
            jnp.zeros((HD + 16, half), f32),
        )
        state = lax.fori_loop(first, clear, functools.partial(step, masked=True), state)
        state = lax.fori_loop(clear, own_block, functools.partial(step, masked=False), state)
        peak, total = step(own_block, state, masked=True)
        row_sum = total[HD : HD + 1]
        mixed_ref[:, lanes] = (total[:HD] / row_sum).astype(bf16)
        log_ref[0, :, lanes] = peak + jnp.log(row_sum)


def split_three(row):
    high = row.astype(bf16)
    rest = row - high.astype(f32)
    mid = rest.astype(bf16)
    low = (rest - mid.astype(f32)).astype(bf16)
    return high, mid, low


def with_rows(rows, row):
    high, mid, low = (part.astype(f32) for part in split_three(row))
    index = lax.broadcasted_iota(jnp.int32, (HD, row.shape[1]), 0)
    tail = jnp.where(index == 0, high, jnp.where(index == 1, mid, jnp.where(index == 2, low, 0.0)))
    return jnp.concatenate([rows, tail.astype(bf16)], axis=0)


def attend_back_kernel(
    info_ref, query_ref, key_ref, value_ref, key_sib_ref, value_sib_ref, start_ref,
    mixed_ref, grad_ref, log_ref,
    own_ref, sib_ref, key_s, value_s, key_t, grad_key_s, grad_value_s,
):
    half = query_ref.shape[1] // 2
    ones_cols = jnp.where(
        lax.broadcasted_iota(jnp.int32, (half, HD), 1) < 3, 1.0, 0.0
    ).astype(bf16)

    def store(sibling, part, block):
        key_from, value_from = (key_sib_ref, value_sib_ref) if sibling else (key_ref, value_ref)
        lanes = slice(part * half, (part + 1) * half)
        key_rows = key_from[:, lanes]
        key_t[block] = key_rows
        key_s[block] = jnp.concatenate([key_rows.astype(f32).T.astype(bf16), ones_cols], axis=1)
        value_s[block] = jnp.concatenate(
            [value_from[:, lanes].astype(f32).T.astype(bf16), ones_cols], axis=1
        )

    place_blocks(info_ref, store)
    grad_key_s[...] = jnp.zeros_like(grad_key_s)
    grad_value_s[...] = jnp.zeros_like(grad_value_s)
    for part in range(2):
        lanes = slice(part * half, (part + 1) * half)
        query = query_ref[:, lanes] * jnp.asarray(score_scale, bf16)
        grad = grad_ref[:, lanes]
        start_row = start_ref[:, lanes]
        delta = jnp.sum(
            grad.astype(f32) * mixed_ref[:, lanes].astype(f32), axis=0, keepdims=True
        )
        query_rows = with_rows(query, -log_ref[0, :, lanes])
        grad_rows = with_rows(grad, -delta)
        query_n = query.astype(f32).T.astype(bf16)
        grad_n = grad.astype(f32).T.astype(bf16)
        own_block = info_ref[part]
        first = info_ref[4 + part]
        clear = info_ref[6 + part]

        def step(
            block, grad_query, masked, query_rows=query_rows, grad_rows=grad_rows,
            query_n=query_n, grad_n=grad_n, start_row=start_row, own_block=own_block,
        ):
            weights = jnp.exp(dot_nn(key_s[block], query_rows))
            if masked:
                weights = jnp.where(
                    allowed_mask(block * TK, own_block * TQ, start_row), weights, 0.0
                )
            grad_score = (weights * dot_nn(value_s[block], grad_rows)).astype(bf16)
            grad_value_s[block] += dot_nn(weights.astype(bf16), grad_n)
            grad_key_s[block] += dot_nn(grad_score, query_n)
            return grad_query + dot_nn(key_t[block], grad_score)

        grad_query = jnp.zeros((HD, half), f32)
        grad_query = lax.fori_loop(first, clear, functools.partial(step, masked=True), grad_query)
        grad_query = lax.fori_loop(
            clear, own_block, functools.partial(step, masked=False), grad_query
        )
        grad_query = step(own_block, grad_query, masked=True)
        own_ref[0, 0, :, lanes] = (grad_query * score_scale).astype(bf16)

    def give(sibling, part, block):
        lanes = slice(part * half, (part + 1) * half)
        key_rows = grad_key_s[block].T.astype(bf16)
        value_rows = grad_value_s[block].T.astype(bf16)
        if sibling:
            sib_ref[0, 0, :, lanes] = key_rows
            sib_ref[1, 0, :, lanes] = value_rows
        else:
            own_ref[1, 0, :, lanes] = key_rows
            own_ref[2, 0, :, lanes] = value_rows

    place_blocks(info_ref, give)


def head_spec(offset, tokens):
    return pl.BlockSpec((HD, tokens), lambda head, info: (head + offset, 0))


head_parts = ((0, 9), (9, 17))
head_parts_back = ((0, 6), (6, 12), (12, 17))


def attend(info, joined, sibling, start_row):
    tokens = joined.shape[1]
    blocks = 2 * tokens // TK
    held = ()
    for first, last in head_parts:
        heads = last - first

        def kernel(info_ref, *refs, skip=len(held)):
            attend_kernel(info_ref, *refs[:6], *refs[6 + skip :])

        held = pl.pallas_call(
            kernel,
            out_shape=(
                jax.ShapeDtypeStruct((D, tokens), bf16),
                jax.ShapeDtypeStruct((H, 1, tokens), f32),
            ),
            grid_spec=pltpu.PrefetchScalarGridSpec(
                num_scalar_prefetch=1,
                grid=(heads,),
                in_specs=[
                    head_spec(first, tokens),
                    head_spec(H + first, tokens),
                    head_spec(2 * H + first, tokens),
                    head_spec(first, tokens),
                    head_spec(H + first, tokens),
                    pl.BlockSpec((1, tokens), lambda head, info: (0, 0)),
                ]
                + [pl.BlockSpec(memory_space=pl.ANY)] * len(held),
                out_specs=(
                    head_spec(first, tokens),
                    pl.BlockSpec((1, 1, tokens), lambda head, info, f=first: (head + f, 0, 0)),
                ),
                scratch_shapes=[
                    pltpu.VMEM((blocks, TK, HD), bf16),
                    pltpu.VMEM((blocks, HD + 16, TK), bf16),
                ],
            ),
            input_output_aliases={7 + i: i for i in range(len(held))},
            compiler_params=pltpu.CompilerParams(vmem_limit_bytes=VMEM_BYTES),
            cost_estimate=pl.CostEstimate(
                flops=heads * 10 * 4 * TK * TQ * 384,
                bytes_accessed=14 * HD * heads * tokens,
                transcendentals=heads * 5 * TK * TQ,
            ),
            name="attend",
        )(info, joined, joined, joined, sibling, sibling, start_row, *held)
    return held


def attend_back(info, joined, sibling, start_row, mixed, grad_mixed, log_total):
    tokens = joined.shape[1]
    blocks = 2 * tokens // TK
    held = ()
    for first, last in head_parts_back:
        heads = last - first

        def kernel(info_ref, *refs, skip=len(held)):
            attend_back_kernel(info_ref, *refs[:9], *refs[9 + skip :])

        held = pl.pallas_call(
            kernel,
            out_shape=(
                jax.ShapeDtypeStruct((3, H, HD, tokens), bf16),
                jax.ShapeDtypeStruct((2, H, HD, tokens), bf16),
            ),
            grid_spec=pltpu.PrefetchScalarGridSpec(
                num_scalar_prefetch=1,
                grid=(heads,),
                in_specs=[
                    head_spec(first, tokens),
                    head_spec(H + first, tokens),
                    head_spec(2 * H + first, tokens),
                    head_spec(first, tokens),
                    head_spec(H + first, tokens),
                    pl.BlockSpec((1, tokens), lambda head, info: (0, 0)),
                    head_spec(first, tokens),
                    head_spec(first, tokens),
                    pl.BlockSpec((1, 1, tokens), lambda head, info, f=first: (head + f, 0, 0)),
                ]
                + [pl.BlockSpec(memory_space=pl.ANY)] * len(held),
                out_specs=(
                    pl.BlockSpec((3, 1, HD, tokens), lambda head, info, f=first: (0, head + f, 0, 0)),
                    pl.BlockSpec((2, 1, HD, tokens), lambda head, info, f=first: (0, head + f, 0, 0)),
                ),
                scratch_shapes=[
                    pltpu.VMEM((blocks, TK, 2 * HD), bf16),
                    pltpu.VMEM((blocks, TK, 2 * HD), bf16),
                    pltpu.VMEM((blocks, HD, TK), bf16),
                    pltpu.VMEM((blocks, TK, HD), f32),
                    pltpu.VMEM((blocks, TK, HD), f32),
                ],
            ),
            input_output_aliases={10 + i: i for i in range(len(held))},
            compiler_params=pltpu.CompilerParams(vmem_limit_bytes=VMEM_BYTES),
            cost_estimate=pl.CostEstimate(
                flops=heads * 10 * 10 * TK * TQ * 256,
                bytes_accessed=30 * HD * heads * tokens,
                transcendentals=heads * 5 * TK * TQ,
            ),
            name="attend_back",
        )(info, joined, joined, joined, sibling, sibling, start_row, mixed, grad_mixed, log_total, *held)
    return held


lines = [(i, (i + 2) % 8) for i in range(8)]
line_hops = [[(i, (i + 2 * hop) % 8) for i in range(8)] for hop in range(4)]
across = [(i, i ^ 1) for i in range(8)]
sibling_pairs = [(i, i ^ 1) for i in range(4)]
far_pairs = [(i, i ^ 2) for i in range(4)]
mirror_pairs = [(i, 3 - i) for i in range(4)]


def half_groups(groups):
    return (groups + 1) // 2


def assemble_kernel(info_ref, *refs, groups, pieces):
    half = half_groups(groups)
    full_ref, extra_ref, stage, in_sems, out_sems = refs[-5:]
    z, x, core = info_ref[0], info_ref[1], info_ref[2]
    slots, come, leave = [], [], []
    for which in range(2 * pieces):
        part = pl.ds((core if which < pieces else 1 - core) * half, half)
        if pieces == 1:
            target = stage.at[:, part]
        else:
            hop, side = which % 4, (which // 4) % 2
            slot = lax.rem(z - hop + 4, 4) * 2 + (1 - x if side else x)
            slots.append(slot)
            target = stage.at[slot, part]
        come.append(pltpu.make_async_copy(refs[which], target, in_sems.at[which]))
    for copy in come:
        copy.start()
    for index in range(8):
        slot = index if pieces == 1 else slots[index]
        if pieces == 1:
            if index == 0:
                come[0].wait()
                come[1].wait()
        else:
            come[index].wait()
            come[index + 8].wait()
        leave.append(
            pltpu.make_async_copy(
                stage.at[slot, pl.ds(0, groups)],
                full_ref.at[pl.ds(slot * groups, groups)],
                out_sems.at[index],
            )
        )
        if 2 * half > groups:
            leave.append(
                pltpu.make_async_copy(
                    stage.at[slot, pl.ds(groups, 1)],
                    extra_ref.at[pl.ds(slot, 1)],
                    out_sems.at[8 + index],
                )
            )
        for copy in leave[-1 if 2 * half == groups else -2 :]:
            copy.start()
    for copy in leave:
        copy.wait()


def assemble(info, pieces, groups, columns):
    any_spec = pl.BlockSpec(memory_space=pl.ANY)
    half = half_groups(groups)
    return pl.pallas_call(
        functools.partial(assemble_kernel, groups=groups, pieces=len(pieces) // 2),
        out_shape=(
            jax.ShapeDtypeStruct((8 * groups, 8, columns), bf16),
            jax.ShapeDtypeStruct((8, 8, columns), bf16),
        ),
        grid_spec=pltpu.PrefetchScalarGridSpec(
            num_scalar_prefetch=1,
            grid=(1,),
            in_specs=[any_spec] * len(pieces),
            out_specs=(any_spec, any_spec),
            scratch_shapes=[
                pltpu.VMEM((8, 2 * half, 8, columns), bf16),
                pltpu.SemaphoreType.DMA((len(pieces),)),
                pltpu.SemaphoreType.DMA((16,)),
            ],
        ),
        compiler_params=pltpu.CompilerParams(vmem_limit_bytes=VMEM_BYTES),
        cost_estimate=pl.CostEstimate(
            flops=0, bytes_accessed=2 * 8 * groups * 8 * columns * 2, transcendentals=0
        ),
        name="assemble",
    )(info, *pieces)


def core_piece(weight, core, extra=None):
    rows, columns = weight.shape
    groups = rows // 8
    half = half_groups(groups)
    grouped = weight.reshape(groups, 8, columns)
    if 2 * half > groups:
        spare = jnp.zeros((1, 8, columns), weight.dtype)
        if extra is not None:
            spare = lax.dynamic_update_slice(spare, extra.reshape(1, 1, -1), (0, 0, 0))
        grouped = jnp.concatenate([grouped, spare], axis=0)
    return lax.dynamic_slice_in_dim(grouped, core * half, half, 0)


def gather_by_lines(weight, info, core, extra=None):
    rows, columns = weight.shape
    piece = core_piece(weight, core, extra)
    line = [piece]
    for _ in range(3):
        line.append(lax.ppermute(line[-1], "dp", lines))
    other = [lax.ppermute(part, "dp", across) for part in line]
    own = line + other
    sib = [lax.ppermute(part, "seq", sibling_pairs) for part in own]
    full, spare = assemble(info, own + sib, rows // 8, columns)
    return full.reshape(8 * rows, columns), spare


def gather_whole(weight, info, core):
    rows, columns = weight.shape
    own = lax.all_gather(core_piece(weight, core), "dp", axis=0)
    sib = lax.ppermute(own, "seq", sibling_pairs)
    full, _ = assemble(info, [own, sib], rows // 8, columns)
    return full.reshape(8 * rows, columns)


def reduce_weight(grad, core, x, z):
    shards = lax.axis_size("dp")
    total_rows, columns = grad.shape
    rows = total_rows // shards
    if shards != 8:
        part = lax.psum_scatter(grad.astype(bf16), "dp", scatter_dimension=0, tiled=True)
        return lax.psum(part, "seq").astype(f32)
    groups = rows // 8
    half = half_groups(groups)
    even = groups - half
    parts = grad.astype(bf16).reshape(4, 2, groups, 8, columns)

    def core_part(which):
        return lax.dynamic_slice_in_dim(parts, which * even, half, 2)

    from_core = lax.ppermute(core_part(1 - core), "seq", sibling_pairs)
    chip = core_part(core).astype(f32) + from_core.astype(f32)
    to_x = lax.dynamic_index_in_dim(chip, 1 - x, 1, keepdims=False).astype(bf16)
    keep_x = lax.dynamic_index_in_dim(chip, x, 1, keepdims=False).astype(bf16)
    from_x = lax.ppermute(to_x, "dp", across)

    def chunk(which):
        mine = lax.dynamic_index_in_dim(keep_x, which, 0, keepdims=False)
        theirs = lax.dynamic_index_in_dim(from_x, which, 0, keepdims=False)
        return mine.astype(f32) + theirs.astype(f32)

    total = chunk(z)
    for hop in range(1, 4):
        sent = chunk(lax.rem(z + hop, 4)).astype(bf16)
        total = total + lax.ppermute(sent, "dp", line_hops[hop]).astype(f32)
    near = total.astype(bf16)
    far = lax.ppermute(near, "seq", far_pairs)
    own = near.astype(f32) + far.astype(f32)
    sib = lax.ppermute(own, "seq", sibling_pairs)
    own = own.reshape(half * 8, columns)
    sib = sib.reshape(half * 8, columns)
    cut = (half - even) * 8
    first = jnp.where(core == 0, own, sib)
    second = jnp.where(core == 0, sib, own)
    return jnp.concatenate([first, second[cut:]], axis=0)


def reduce_small(rows, x, z):
    shards = rows.shape[0]
    if shards != 8:
        part = lax.psum_scatter(rows, "dp", scatter_dimension=0)
        return lax.psum(part, "seq")
    total = rows + lax.ppermute(rows, "seq", sibling_pairs)
    total = total + lax.ppermute(total, "seq", far_pairs)
    parts = total.reshape((4, 2) + total.shape[1:])
    keep = lax.dynamic_index_in_dim(parts, x, 1, keepdims=False)
    give = lax.dynamic_index_in_dim(parts, 1 - x, 1, keepdims=False)
    keep = keep + lax.ppermute(give, "dp", across)

    def chunk(which):
        return lax.dynamic_index_in_dim(keep, which, 0, keepdims=False)

    out = chunk(z)
    for hop in range(1, 4):
        out = out + lax.ppermute(chunk(lax.rem(z + hop, 4)), "dp", line_hops[hop])
    return out


def body(
    tokens,
    qkv_weight,
    out_weight,
    up_weight,
    down_weight,
    norm_gain,
    norm_shift,
    bias_rows,
    bias_hidden,
    doc_lengths,
    cotangent,
):
    block_rows = tokens.shape[1]
    length = block_rows * lax.axis_size("seq")
    shard = tokens.shape[2] // lax.axis_size("dp")
    own = lax.axis_index("seq")
    dp_index = lax.axis_index("dp")
    core = own % 2
    kept = own // 2
    z, x = dp_index // 2, dp_index % 2
    place = jnp.stack([z, x, core]).astype(jnp.int32)

    small = jnp.concatenate(
        [norm_gain, norm_shift, bias_rows, bias_hidden.reshape(4, shard)], axis=0
    )
    if lax.axis_size("dp") == 8:
        qkv_full, spare = gather_by_lines(qkv_weight, place, core, small)
        small_all = spare[:, 0, : small.size].reshape(8, 12, shard).astype(f32)
        out_full, _ = gather_by_lines(out_weight, place, core)
        up_full = gather_whole(up_weight, place, core)
        down_full = gather_whole(down_weight, place, core)
    else:
        small_all = lax.all_gather(small, "dp", axis=0).astype(f32)
        qkv_full, out_full, up_full, down_full = (
            lax.all_gather(weight, "dp", axis=0, tiled=True)
            for weight in (qkv_weight, out_weight, up_weight, down_weight)
        )
    small_rows = jnp.transpose(small_all[:, :8], (1, 0, 2)).reshape(8, D)
    small_cols = small_rows.T
    gain_one, gain_two = small_cols[:, 0:1], small_cols[:, 1:2]
    shift_one, shift_two = small_cols[:, 2:3], small_cols[:, 3:4]
    bias_query, bias_value = small_cols[:, 4:5], small_cols[:, 5:6]
    bias_out, bias_down = small_cols[:, 6:7], small_cols[:, 7:8]
    bias_up = small_all[:, 8:].reshape(FF, 1)

    def take(rows):
        cols = jnp.transpose(rows, (0, 2, 1))
        keep = lax.dynamic_index_in_dim(cols, kept, 0, keepdims=False)
        give = lax.dynamic_index_in_dim(cols, 1 - kept, 0, keepdims=False)
        return jnp.concatenate([keep, lax.ppermute(give, "seq", mirror_pairs)], axis=1)

    def give_back(cols, dtype):
        keep = cols[:, :block_rows]
        got = lax.ppermute(cols[:, block_rows:].astype(bf16), "seq", mirror_pairs)
        keep, got = keep.astype(dtype), got.astype(dtype)
        first = jnp.where(kept == 0, keep, got)
        second = jnp.where(kept == 0, got, keep)
        return jnp.transpose(jnp.stack([first, second]), (0, 2, 1))

    x_in = take(tokens)
    cot = take(cotangent)

    lengths = lax.dynamic_index_in_dim(doc_lengths, kept, 0, keepdims=False)
    bounds = jnp.cumsum(lengths)[:-1].astype(jnp.int32)
    mirror = 3 - own
    inside = jnp.arange(block_rows, dtype=jnp.int32)
    positions = jnp.concatenate([own * block_rows + inside, mirror * block_rows + inside])
    starts = jnp.max(jnp.where(bounds[:, None] <= positions[None, :], bounds[:, None], 0), axis=0)
    firsts = jnp.stack([starts[0], starts[block_rows]]) // TK
    lasts = jnp.stack([starts[block_rows - 1], starts[2 * block_rows - 1]])
    own_blocks = jnp.stack([own, mirror])
    clears = jnp.minimum((lasts + TK - 1) // TK, own_blocks)
    near = own ^ 1
    info = jnp.concatenate(
        [own_blocks, jnp.stack([near, 3 - near]), jnp.minimum(firsts, clears), clears]
    ).astype(jnp.int32)
    start_row = starts[None, :]

    x_float = x_in.astype(f32)
    unit_one, inverse_one = norm_stats(x_float)
    normed = (unit_one * gain_one + shift_one).astype(bf16)
    joined_bias = jnp.concatenate([bias_query, jnp.zeros_like(bias_query), bias_value], axis=0)
    joined = (dot_tn(qkv_full, normed) + joined_bias).astype(bf16)
    sibling = lax.ppermute(joined[D:], "seq", sibling_pairs)
    mixed, log_total = attend(info, joined, sibling, start_row)
    residual = x_float + dot_tn(out_full, mixed) + bias_out
    unit_two, inverse_two = norm_stats(residual)
    normed_two = (unit_two * gain_two + shift_two).astype(bf16)
    up_proj = dot_tn(up_full, normed_two) + bias_up
    active, slope_of = jax.vjp(lambda pre: jax.nn.gelu(pre, approximate=True), up_proj)
    slope = slope_of(jnp.ones_like(up_proj))[0].astype(bf16)
    active = active.astype(bf16)
    layer_cols = residual + dot_tn(down_full, active) + bias_down
    layer_out = give_back(layer_cols, bf16)

    cot_float = cot.astype(f32)
    grad_down = reduce_weight(dot_nt(active, cot).astype(bf16), core, x, z)
    grad_up_proj = (dot_nn(down_full, cot) * slope.astype(f32)).astype(bf16)
    grad_up = reduce_weight(dot_nt(normed_two, grad_up_proj).astype(bf16), core, x, z)
    grad_hidden = jnp.sum(grad_up_proj.astype(f32), axis=1)
    grad_a2 = dot_nn(up_full, grad_up_proj)
    grad_gain_two = jnp.sum(grad_a2 * unit_two, axis=1)
    grad_shift_two = jnp.sum(grad_a2, axis=1)
    grad_residual = cot_float + norm_back(grad_a2, unit_two, inverse_two, gain_two)
    grad_branch = grad_residual.astype(bf16)

    grad_out = reduce_weight(dot_nt(mixed, grad_branch).astype(bf16), core, x, z)
    grad_mixed = dot_nn(out_full, grad_branch).astype(bf16)
    own_grads, sib_grads = attend_back(
        info, joined, sibling, start_row, mixed, grad_mixed, log_total
    )
    tokens_here = x_in.shape[1]
    own_grads = own_grads.reshape(3 * D, tokens_here)
    from_sib = lax.ppermute(sib_grads.reshape(2 * D, tokens_here), "seq", sibling_pairs)
    grad_joined = jnp.concatenate(
        [own_grads[:D], (own_grads[D:].astype(f32) + from_sib.astype(f32)).astype(bf16)], axis=0
    )
    grad_qkv = reduce_weight(dot_nt(normed, grad_joined).astype(bf16), core, x, z)
    joined_sums = jnp.sum(grad_joined.astype(f32), axis=1)
    grad_a1 = dot_nn(qkv_full, grad_joined)
    grad_gain_one = jnp.sum(grad_a1 * unit_one, axis=1)
    grad_shift_one = jnp.sum(grad_a1, axis=1)
    grad_x = grad_residual + norm_back(grad_a1, unit_one, inverse_one, gain_one)
    grad_tokens = give_back(grad_x, f32)

    small_grads = jnp.stack(
        [
            grad_gain_one,
            grad_gain_two,
            grad_shift_one,
            grad_shift_two,
            joined_sums[:D],
            joined_sums[2 * D :],
            jnp.sum(grad_branch.astype(f32), axis=1),
            jnp.sum(cot_float, axis=1),
        ]
    )
    shards = lax.axis_size("dp")
    small_parts = jnp.concatenate(
        [
            jnp.transpose(small_grads.reshape(8, shards, shard), (1, 0, 2)),
            grad_hidden.reshape(shards, 4, shard),
        ],
        axis=1,
    )
    small_own = reduce_small(small_parts, x, z)
    hidden_own = small_own[8:].reshape(4 * shard)

    return (
        layer_out,
        grad_tokens,
        grad_qkv,
        grad_out,
        grad_up,
        grad_down,
        small_own[0:2],
        small_own[2:4],
        small_own[4:8],
        hidden_own,
    )


def solution(mesh):
    placed = (
        P("dp", "seq", None),
        P("dp", None),
        P("dp", None),
        P("dp", None),
        P("dp", None),
        P(None, "dp"),
        P(None, "dp"),
        P(None, "dp"),
        P("dp"),
        P("dp", None),
        P("dp", "seq", None),
    )
    return jax.shard_map(
        body,
        mesh=mesh,
        in_specs=placed,
        out_specs=(
            P("dp", "seq", None),
            P("dp", "seq", None),
            P("dp", None),
            P("dp", None),
            P("dp", None),
            P("dp", None),
            P(None, "dp"),
            P(None, "dp"),
            P(None, "dp"),
            P("dp"),
        ),
        check_vma=False,
    )
```

```python
import functools

import jax
import jax.numpy as jnp
from jax import lax
from jax.experimental import pallas as pl
from jax.experimental.layout import Layout, with_layout_constraint
from jax.experimental.pallas import tpu as pltpu
from jax.sharding import PartitionSpec as P

D = 1088
H = 17
HD = 64
FF = 4352

norm_eps = 1e-05
masked_score = -1e30
score_scale = HD ** (-0.5)

TQ = 512
TK = 512
VMEM_BYTES = 56 * 1024 * 1024

f32 = jnp.float32
bf16 = jnp.bfloat16


def dot_tn(left, right):
    return lax.dot_general(left, right, (((0,), (0,)), ((), ())), preferred_element_type=f32)


def dot_nn(left, right):
    return lax.dot_general(left, right, (((1,), (0,)), ((), ())), preferred_element_type=f32)


def dot_nt(left, right):
    return lax.dot_general(left, right, (((1,), (1,)), ((), ())), preferred_element_type=f32)


def after(value, *others):
    return lax.optimization_barrier((value,) + others)[0]


def by_rows(value):
    return with_layout_constraint(value, Layout(major_to_minor=(0, 1)))


def norm_stats(rows):
    centre = rows - jnp.mean(rows, axis=0, keepdims=True)
    spread = jnp.mean(centre * centre, axis=0, keepdims=True)
    inverse = lax.rsqrt(spread + norm_eps)
    return centre * inverse, inverse


def norm_back(grad, unit, inverse, gain):
    scaled = grad * gain
    mean_one = jnp.mean(scaled, axis=0, keepdims=True)
    mean_two = jnp.mean(scaled * unit, axis=0, keepdims=True)
    return inverse * (scaled - mean_one - unit * mean_two)


def place_blocks(info_ref, store):
    for which in range(4):
        store(which // 2, which % 2, info_ref[which])


def allowed_mask(key_first, query_first, start_row):
    shape = (TK, TQ)
    key_pos = key_first + lax.broadcasted_iota(jnp.int32, shape, 0)
    query_pos = query_first + lax.broadcasted_iota(jnp.int32, shape, 1)
    return (key_pos <= query_pos) & (key_pos >= start_row)


def attend_kernel(
    info_ref, query_ref, key_ref, value_ref, key_sib_ref, value_sib_ref, start_ref,
    mixed_ref, log_ref, key_s, value_s,
):
    half = query_ref.shape[1] // 2
    ones_rows = jnp.ones((16, half), bf16)

    def store(sibling, part, block):
        key_from, value_from = (key_sib_ref, value_sib_ref) if sibling else (key_ref, value_ref)
        lanes = slice(part * half, (part + 1) * half)
        key_s[block] = key_from[:, lanes].astype(f32).T.astype(bf16)
        value_s[block] = jnp.concatenate([value_from[:, lanes], ones_rows], axis=0)

    place_blocks(info_ref, store)
    for part in range(2):
        lanes = slice(part * half, (part + 1) * half)
        query = query_ref[:, lanes] * jnp.asarray(score_scale, bf16)
        start_row = start_ref[:, lanes]
        own_block = info_ref[part]
        first = info_ref[4 + part]
        clear = info_ref[6 + part]

        def step(block, state, masked, query=query, start_row=start_row, own_block=own_block):
            peak, total = state
            scores = dot_nn(key_s[block], query)
            if masked:
                scores = jnp.where(
                    allowed_mask(block * TK, own_block * TQ, start_row), scores, masked_score
                )
            new_peak = jnp.maximum(peak, jnp.max(scores, axis=0, keepdims=True))
            weights = jnp.exp(scores - new_peak).astype(bf16)
            total = total * jnp.exp(peak - new_peak) + dot_nn(value_s[block], weights)
            return new_peak, total

        state = (
            jnp.full((1, half), masked_score, f32),
            jnp.zeros((HD + 16, half), f32),
        )
        state = lax.fori_loop(first, clear, functools.partial(step, masked=True), state)
        state = lax.fori_loop(clear, own_block, functools.partial(step, masked=False), state)
        peak, total = step(own_block, state, masked=True)
        row_sum = total[HD : HD + 1]
        mixed_ref[:, lanes] = (total[:HD] / row_sum).astype(bf16)
        log_ref[0, :, lanes] = peak + jnp.log(row_sum)


def split_three(row):
    high = row.astype(bf16)
    rest = row - high.astype(f32)
    mid = rest.astype(bf16)
    low = (rest - mid.astype(f32)).astype(bf16)
    return high, mid, low


def with_rows(rows, row):
    high, mid, low = (part.astype(f32) for part in split_three(row))
    index = lax.broadcasted_iota(jnp.int32, (HD, row.shape[1]), 0)
    tail = jnp.where(index == 0, high, jnp.where(index == 1, mid, jnp.where(index == 2, low, 0.0)))
    return jnp.concatenate([rows, tail.astype(bf16)], axis=0)


def attend_back_kernel(
    info_ref, query_ref, key_ref, value_ref, key_sib_ref, value_sib_ref, start_ref,
    mixed_ref, grad_ref, log_ref,
    own_ref, sib_ref, key_s, value_s, key_t, grad_key_s, grad_value_s,
):
    half = query_ref.shape[1] // 2
    ones_cols = jnp.where(
        lax.broadcasted_iota(jnp.int32, (half, HD), 1) < 3, 1.0, 0.0
    ).astype(bf16)

    def store(sibling, part, block):
        key_from, value_from = (key_sib_ref, value_sib_ref) if sibling else (key_ref, value_ref)
        lanes = slice(part * half, (part + 1) * half)
        key_rows = key_from[:, lanes]
        key_t[block] = key_rows
        key_s[block] = jnp.concatenate([key_rows.astype(f32).T.astype(bf16), ones_cols], axis=1)
        value_s[block] = jnp.concatenate(
            [value_from[:, lanes].astype(f32).T.astype(bf16), ones_cols], axis=1
        )

    place_blocks(info_ref, store)
    grad_key_s[...] = jnp.zeros_like(grad_key_s)
    grad_value_s[...] = jnp.zeros_like(grad_value_s)
    for part in range(2):
        lanes = slice(part * half, (part + 1) * half)
        query = query_ref[:, lanes] * jnp.asarray(score_scale, bf16)
        grad = grad_ref[:, lanes]
        start_row = start_ref[:, lanes]
        delta = jnp.sum(
            grad.astype(f32) * mixed_ref[:, lanes].astype(f32), axis=0, keepdims=True
        )
        query_rows = with_rows(query, -log_ref[0, :, lanes])
        grad_rows = with_rows(grad, -delta)
        query_n = query.astype(f32).T.astype(bf16)
        grad_n = grad.astype(f32).T.astype(bf16)
        own_block = info_ref[part]
        first = info_ref[4 + part]
        clear = info_ref[6 + part]

        def step(
            block, grad_query, masked, query_rows=query_rows, grad_rows=grad_rows,
            query_n=query_n, grad_n=grad_n, start_row=start_row, own_block=own_block,
        ):
            weights = jnp.exp(dot_nn(key_s[block], query_rows))
            if masked:
                weights = jnp.where(
                    allowed_mask(block * TK, own_block * TQ, start_row), weights, 0.0
                )
            grad_score = (weights * dot_nn(value_s[block], grad_rows)).astype(bf16)
            grad_value_s[block] += dot_nn(weights.astype(bf16), grad_n)
            grad_key_s[block] += dot_nn(grad_score, query_n)
            return grad_query + dot_nn(key_t[block], grad_score)

        grad_query = jnp.zeros((HD, half), f32)
        grad_query = lax.fori_loop(first, clear, functools.partial(step, masked=True), grad_query)
        grad_query = lax.fori_loop(
            clear, own_block, functools.partial(step, masked=False), grad_query
        )
        grad_query = step(own_block, grad_query, masked=True)
        own_ref[0, 0, :, lanes] = (grad_query * score_scale).astype(bf16)

    def give(sibling, part, block):
        lanes = slice(part * half, (part + 1) * half)
        key_rows = grad_key_s[block].T.astype(bf16)
        value_rows = grad_value_s[block].T.astype(bf16)
        if sibling:
            sib_ref[0, 0, :, lanes] = key_rows
            sib_ref[1, 0, :, lanes] = value_rows
        else:
            own_ref[1, 0, :, lanes] = key_rows
            own_ref[2, 0, :, lanes] = value_rows

    place_blocks(info_ref, give)


def head_spec(offset, tokens):
    return pl.BlockSpec((HD, tokens), lambda head, info: (head + offset, 0))


def attend(info, joined, sibling, start_row, first, last, held=()):
    tokens = joined.shape[1]
    blocks = 2 * tokens // TK
    heads = last - first

    def kernel(info_ref, *refs):
        attend_kernel(info_ref, *refs[:6], *refs[6 + len(held) :])

    return pl.pallas_call(
        kernel,
        out_shape=(
            jax.ShapeDtypeStruct((D, tokens), bf16),
            jax.ShapeDtypeStruct((H, 1, tokens), f32),
        ),
        grid_spec=pltpu.PrefetchScalarGridSpec(
            num_scalar_prefetch=1,
            grid=(heads,),
            in_specs=[
                head_spec(first, tokens),
                head_spec(H + first, tokens),
                head_spec(2 * H + first, tokens),
                head_spec(first, tokens),
                head_spec(H + first, tokens),
                pl.BlockSpec((1, tokens), lambda head, info: (0, 0)),
            ]
            + [pl.BlockSpec(memory_space=pl.ANY)] * len(held),
            out_specs=(
                head_spec(first, tokens),
                pl.BlockSpec((1, 1, tokens), lambda head, info: (head + first, 0, 0)),
            ),
            scratch_shapes=[
                pltpu.VMEM((blocks, TK, HD), bf16),
                pltpu.VMEM((blocks, HD + 16, TK), bf16),
            ],
        ),
        input_output_aliases={7 + i: i for i in range(len(held))},
        compiler_params=pltpu.CompilerParams(vmem_limit_bytes=VMEM_BYTES),
        cost_estimate=pl.CostEstimate(
            flops=10**6, bytes_accessed=10**5, transcendentals=0
        ),
        name="attend",
    )(info, joined, joined, joined, sibling, sibling, start_row, *held)


def attend_back(
    info, joined, sibling, start_row, mixed, grad_mixed, log_total, first, last, held=()
):
    tokens = joined.shape[1]
    blocks = 2 * tokens // TK
    heads = last - first

    def kernel(info_ref, *refs):
        attend_back_kernel(info_ref, *refs[:9], *refs[9 + len(held) :])

    return pl.pallas_call(
        kernel,
        out_shape=(
            jax.ShapeDtypeStruct((3, H, HD, tokens), bf16),
            jax.ShapeDtypeStruct((2, heads, HD, tokens), bf16),
        ),
        grid_spec=pltpu.PrefetchScalarGridSpec(
            num_scalar_prefetch=1,
            grid=(heads,),
            in_specs=[
                head_spec(first, tokens),
                head_spec(H + first, tokens),
                head_spec(2 * H + first, tokens),
                head_spec(first, tokens),
                head_spec(H + first, tokens),
                pl.BlockSpec((1, tokens), lambda head, info: (0, 0)),
                head_spec(first, tokens),
                head_spec(first, tokens),
                pl.BlockSpec((1, 1, tokens), lambda head, info: (head + first, 0, 0)),
            ]
            + [pl.BlockSpec(memory_space=pl.ANY)] * len(held),
            out_specs=(
                pl.BlockSpec((3, 1, HD, tokens), lambda head, info: (0, head + first, 0, 0)),
                pl.BlockSpec((2, 1, HD, tokens), lambda head, info: (0, head, 0, 0)),
            ),
            scratch_shapes=[
                pltpu.VMEM((blocks, TK, 2 * HD), bf16),
                pltpu.VMEM((blocks, TK, 2 * HD), bf16),
                pltpu.VMEM((blocks, HD, TK), bf16),
                pltpu.VMEM((blocks, TK, HD), f32),
                pltpu.VMEM((blocks, TK, HD), f32),
            ],
        ),
        input_output_aliases={10 + i: i for i in range(len(held))},
        compiler_params=pltpu.CompilerParams(vmem_limit_bytes=VMEM_BYTES),
        cost_estimate=pl.CostEstimate(
            flops=10**6, bytes_accessed=10**5, transcendentals=0
        ),
        name="attend_back",
    )(info, joined, joined, joined, sibling, sibling, start_row, mixed, grad_mixed, log_total, *held)


lines = [(i, (i + 2) % 8) for i in range(8)]
line_hops = [[(i, (i + 2 * hop) % 8) for i in range(8)] for hop in range(4)]
across = [(i, i ^ 1) for i in range(8)]
sibling_pairs = [(i, i ^ 1) for i in range(4)]
far_pairs = [(i, i ^ 2) for i in range(4)]
mirror_pairs = [(i, 3 - i) for i in range(4)]


def half_groups(groups):
    return (groups + 1) // 2


def assemble_kernel(info_ref, *refs, groups, half, pieces, by_columns):
    full_ref, extra_ref, stage, in_sems, out_sems = refs[-5:]
    z, x, core, far = info_ref[0], info_ref[1], info_ref[2], info_ref[3]
    slots, come, leave = list(range(8)), [], []
    for which in range(pieces):
        if pieces == 16:
            part = pl.ds((core if which < 8 else 1 - core) * half, half)
            hop, side = which % 4, (which // 4) % 2
            slot = lax.rem(z - hop + 4, 4) * 2 + (1 - x if side else x)
            if which < 8:
                slots[which] = slot
            target = stage.at[slot, part]
        else:
            side = core if which % 2 == 0 else 1 - core
            plane = far if which < 2 else 1 - far
            if pieces == 2:
                target = stage.at[:, pl.ds(side * half, half)]
            elif by_columns:
                width = stage.shape[3] // 2
                lanes = pl.ds(pl.multiple_of(plane * width, 128), width)
                target = stage.at[:, pl.ds(side * half, half), :, lanes]
            else:
                target = stage.at[:, pl.ds((plane * 2 + side) * half, half)]
        come.append(pltpu.make_async_copy(refs[which], target, in_sems.at[which]))
    for copy in come:
        copy.start()
    if pieces < 16:
        for copy in come:
            copy.wait()
    for index in range(8):
        slot = slots[index]
        if pieces == 16:
            come[index].wait()
            come[index + 8].wait()
        out = [
            pltpu.make_async_copy(
                stage.at[slot, pl.ds(0, groups)],
                full_ref.at[pl.ds(slot * groups, groups)],
                out_sems.at[index],
            )
        ]
        if pieces == 16:
            out.append(
                pltpu.make_async_copy(
                    stage.at[slot, pl.ds(groups, 1)],
                    extra_ref.at[pl.ds(slot, 1)],
                    out_sems.at[8 + index],
                )
            )
        for copy in out:
            copy.start()
        leave += out
    for copy in leave:
        copy.wait()


def assemble(info, pieces, groups, columns, by_columns=False):
    any_spec = pl.BlockSpec(memory_space=pl.ANY)
    half = pieces[0].shape[-3]
    staged = groups + groups % 2
    return pl.pallas_call(
        functools.partial(
            assemble_kernel, groups=groups, half=half, pieces=len(pieces), by_columns=by_columns
        ),
        out_shape=(
            jax.ShapeDtypeStruct((8 * groups, 8, columns), bf16),
            jax.ShapeDtypeStruct((8, 8, columns), bf16),
        ),
        grid_spec=pltpu.PrefetchScalarGridSpec(
            num_scalar_prefetch=1,
            grid=(1,),
            in_specs=[any_spec] * len(pieces),
            out_specs=(any_spec, any_spec),
            scratch_shapes=[
                pltpu.VMEM((8, staged, 8, columns), bf16),
                pltpu.SemaphoreType.DMA((len(pieces),)),
                pltpu.SemaphoreType.DMA((16,)),
            ],
        ),
        compiler_params=pltpu.CompilerParams(vmem_limit_bytes=VMEM_BYTES),
        cost_estimate=pl.CostEstimate(
            flops=0, bytes_accessed=10**5, transcendentals=0
        ),
        name="assemble",
    )(info, *pieces)


def core_piece(weight, core, extra=None):
    rows, columns = weight.shape
    groups = rows // 8
    half = half_groups(groups)
    grouped = weight.reshape(groups, 8, columns)
    if 2 * half > groups:
        spare = jnp.zeros((1, 8, columns), weight.dtype)
        if extra is not None:
            spare = lax.dynamic_update_slice(spare, extra.reshape(1, 1, -1), (0, 0, 0))
        grouped = jnp.concatenate([grouped, spare], axis=0)
    return lax.dynamic_slice_in_dim(grouped, core * half, half, 0)


def along_line(piece):
    line = [piece]
    for _ in range(3):
        line.append(lax.ppermute(line[-1], "dp", lines))
    return line


def from_all(piece):
    groups, _, columns = piece.shape
    flat = lax.all_gather(piece.reshape(groups * 8, columns), "dp", axis=0, tiled=True)
    return flat.reshape(8, groups, 8, columns)


def from_across(parts):
    return [lax.ppermute(part, "dp", across) for part in parts]


def from_sibling(parts):
    return [lax.ppermute(part, "seq", sibling_pairs) for part in parts]


def whole(info, weight, pieces, by_columns=False):
    rows, columns = weight.shape
    full, spare = assemble(info, pieces, rows // 8, columns, by_columns)
    return full.reshape(8 * rows, columns), spare


def whole_of_quarters(info, weight, near, far, by_columns=False):
    near_sib, far_sib = from_sibling([near, far])
    return whole(info, weight, [near, near_sib, far, far_sib], by_columns)[0]


class GradSum:
    def __init__(self, grad, place, kind, extra=None):
        self.z, self.x, self.core, self.plane = place
        self.shards = lax.axis_size("dp")
        self.rows = grad.shape[0] // self.shards
        self.columns = grad.shape[1]
        self.kind = kind
        grad = grad.astype(bf16)
        self.stage = 0
        self.extra = extra
        self.operand = grad
        if self.shards == 8:
            groups = self.rows // 8
            parts = grad.reshape(8, groups, 8, self.columns)
            if kind == "rows":
                self.half = self.even = groups // 4
                parts = parts.reshape(8, 2, groups // 2, 8, self.columns)
            else:
                self.half = half_groups(groups)
                self.even = groups - self.half
            if kind == "hops":
                if extra is not None:
                    below = jnp.pad(extra.astype(bf16)[:, None, None, :], ((0, 0), (0, 0), (0, 7), (0, 0)))
                    parts = jnp.concatenate([parts, below], axis=1)
                    self.even = self.half
                parts = parts.reshape((4, 2) + parts.shape[1:])
            self.parts = parts
            self.operand = self.core_part(1 - self.core)

    def core_part(self, which):
        axis = self.parts.ndim - 3
        return lax.dynamic_slice_in_dim(self.parts, which * self.even, self.half, axis)

    def chunk(self, which):
        mine = lax.dynamic_index_in_dim(self.keep, which, 0, keepdims=False)
        theirs = lax.dynamic_index_in_dim(self.came, which, 0, keepdims=False)
        return mine.astype(f32) + theirs.astype(f32)

    def plane_part(self, value, which):
        if self.kind == "rows":
            return lax.dynamic_index_in_dim(value, which, 1, keepdims=False)
        width = self.columns // 2
        return lax.dynamic_slice_in_dim(value, which * width, width, 3)

    def move(self, *beside):
        self.stage += 1
        if self.shards != 8:
            if self.stage == 5:
                part = lax.psum_scatter(self.operand, "dp", scatter_dimension=0, tiled=True)
                self.operand = lax.psum(part, "seq").astype(f32)
                if self.extra is not None:
                    self.extra = lax.psum_scatter(self.extra, "dp", scatter_dimension=0)
                    self.extra = lax.psum(self.extra, "seq")
            return
        core, x, z, plane = self.core, self.x, self.z, self.plane
        hops = self.kind == "hops"

        def arrived(value):
            return after(value, *beside) if beside else value

        if self.stage == 1:
            from_core = arrived(lax.ppermute(self.operand, "seq", sibling_pairs))
            chip = self.core_part(core).astype(f32) + from_core.astype(f32)
            if hops:
                self.operand = lax.dynamic_index_in_dim(chip, 1 - x, 1, keepdims=False).astype(bf16)
                self.keep = lax.dynamic_index_in_dim(chip, x, 1, keepdims=False).astype(bf16)
            elif self.kind == "plain":
                self.operand = chip.astype(bf16)
            else:
                self.operand = self.plane_part(chip, 1 - plane).astype(bf16)
                self.keep = self.plane_part(chip, plane).astype(bf16)
        elif self.stage == 2:
            if hops:
                self.came = arrived(lax.ppermute(self.operand, "dp", across))
                self.operand = [
                    self.chunk(lax.rem(z + hop, 4)).astype(bf16) for hop in range(1, 4)
                ]
            elif self.kind != "plain":
                came = arrived(lax.ppermute(self.operand, "seq", far_pairs))
                self.operand = (self.keep.astype(f32) + came.astype(f32)).astype(bf16)
        elif self.stage == 3:
            if hops:
                moved = arrived(
                    [
                        lax.ppermute(self.operand[hop - 1], "dp", line_hops[hop])
                        for hop in range(1, 4)
                    ]
                )
                total = self.chunk(z)
                for part in moved:
                    total = total + part.astype(f32)
                self.operand = total.astype(bf16)
            else:
                columns = self.operand.shape[-1]
                flat = self.operand.reshape(-1, columns)
                self.operand = arrived(
                    lax.psum_scatter(flat, "dp", scatter_dimension=0, tiled=True)
                )
        elif self.stage == 4:
            far = arrived(lax.ppermute(self.operand, "seq", far_pairs))
            if hops or self.kind == "plain":
                self.operand = (self.operand.astype(f32) + far.astype(f32)).astype(bf16)
            else:
                first = jnp.where(plane == 0, self.operand, far)
                second = jnp.where(plane == 0, far, self.operand)
                axis = 1 if self.kind == "columns" else 0
                self.operand = jnp.stack([first, second]) if axis == 0 else jnp.concatenate([first, second], axis=1)
        else:
            own = self.operand
            sib = arrived(lax.ppermute(own, "seq", sibling_pairs))
            if self.kind == "rows":
                first = jnp.where(core == 0, own, sib)
                second = jnp.where(core == 0, sib, own)
                both = jnp.stack([first, second], axis=1)
                self.operand = both.reshape(self.rows, self.columns).astype(f32)
            else:
                own = own.reshape(self.half * 8, self.columns)
                sib = sib.reshape(self.half * 8, self.columns)
                first = jnp.where(core == 0, own, sib)
                second = jnp.where(core == 0, sib, own)
                cut = (self.half - self.even) * 8
                both = jnp.concatenate([first, second[cut:]], axis=0).astype(f32)
                self.operand = both[: self.rows]
                if self.extra is not None:
                    self.extra = both[self.rows]


def body(
    tokens,
    qkv_weight,
    out_weight,
    up_weight,
    down_weight,
    norm_gain,
    norm_shift,
    bias_rows,
    bias_hidden,
    doc_lengths,
    cotangent,
):
    block_rows = tokens.shape[1]
    length = block_rows * lax.axis_size("seq")
    shard = tokens.shape[2] // lax.axis_size("dp")
    own = lax.axis_index("seq")
    dp_index = lax.axis_index("dp")
    core = own % 2
    kept = own // 2
    z, x = dp_index // 2, dp_index % 2
    place = jnp.stack([z, x, core, kept]).astype(jnp.int32)
    where = (z, x, core, kept)

    small = jnp.concatenate(
        [norm_gain, norm_shift, bias_rows, bias_hidden.reshape(4, shard)], axis=0
    )
    eight = lax.axis_size("dp") == 8
    if eight:
        qkv_line = along_line(core_piece(qkv_weight, core, small))
        qkv_own = qkv_line + from_across(qkv_line)
        qkv_full, spare = whole(place, qkv_weight, qkv_own + from_sibling(qkv_own))
        small_all = spare[:, 0, : small.size].reshape(8, 12, shard).astype(f32)
        up_part = lax.dynamic_slice_in_dim(core_piece(up_weight, core), kept * (FF // 2), FF // 2, 2)
        both_part = jnp.concatenate([up_part, core_piece(out_weight, core)], axis=2)
        both_near = from_all(after(both_part, qkv_line[2]))
        quarter = down_weight.shape[0] // 4
        down_part = lax.dynamic_slice_in_dim(down_weight, own * quarter, quarter, 0)
        down_near = from_all(after(down_part.reshape(-1, 8, D), qkv_own[5]))
    else:
        small_all = lax.all_gather(small, "dp", axis=0).astype(f32)
        qkv_full, out_full, up_full, down_full = (
            lax.all_gather(weight, "dp", axis=0, tiled=True)
            for weight in (qkv_weight, out_weight, up_weight, down_weight)
        )
    small_rows = jnp.transpose(small_all[:, :8], (1, 0, 2)).reshape(8, D)
    small_cols = small_rows.T
    gain_one, gain_two = small_cols[:, 0:1], small_cols[:, 1:2]
    shift_one, shift_two = small_cols[:, 2:3], small_cols[:, 3:4]
    bias_query, bias_value = small_cols[:, 4:5], small_cols[:, 5:6]
    bias_out, bias_down = small_cols[:, 6:7], small_cols[:, 7:8]
    bias_up = small_all[:, 8:].reshape(FF, 1)

    def take(rows):
        cols = jnp.transpose(rows, (0, 2, 1))
        keep = lax.dynamic_index_in_dim(cols, kept, 0, keepdims=False)
        give = lax.dynamic_index_in_dim(cols, 1 - kept, 0, keepdims=False)
        return jnp.concatenate([keep, lax.ppermute(give, "seq", mirror_pairs)], axis=1)

    def give_back(cols, dtype, beside=()):
        keep = cols[:, :block_rows]
        got = lax.ppermute(cols[:, block_rows:].astype(bf16), "seq", mirror_pairs)
        got = after(got, beside)
        keep, got = keep.astype(dtype), got.astype(dtype)
        first = jnp.where(kept == 0, keep, got)
        second = jnp.where(kept == 0, got, keep)
        return jnp.transpose(jnp.stack([first, second]), (0, 2, 1))

    x_in = take(tokens)
    cot = take(cotangent)

    lengths = lax.dynamic_index_in_dim(doc_lengths, kept, 0, keepdims=False)
    bounds = jnp.cumsum(lengths)[:-1].astype(jnp.int32)
    mirror = 3 - own
    inside = jnp.arange(block_rows, dtype=jnp.int32)
    positions = jnp.concatenate([own * block_rows + inside, mirror * block_rows + inside])
    starts = jnp.max(jnp.where(bounds[:, None] <= positions[None, :], bounds[:, None], 0), axis=0)
    firsts = jnp.stack([starts[0], starts[block_rows]]) // TK
    lasts = jnp.stack([starts[block_rows - 1], starts[2 * block_rows - 1]])
    own_blocks = jnp.stack([own, mirror])
    clears = jnp.minimum((lasts + TK - 1) // TK, own_blocks)
    near = own ^ 1
    info = jnp.concatenate(
        [own_blocks, jnp.stack([near, 3 - near]), jnp.minimum(firsts, clears), clears]
    ).astype(jnp.int32)
    start_row = starts[None, :]

    x_float = x_in.astype(f32)
    unit_one, inverse_one = norm_stats(x_float)
    normed = (unit_one * gain_one + shift_one).astype(bf16)
    joined_bias = jnp.concatenate([bias_query, jnp.zeros_like(bias_query), bias_value], axis=0)
    joined = (dot_tn(qkv_full, normed) + joined_bias).astype(bf16)
    sibling = lax.ppermute(joined[D:], "seq", sibling_pairs)
    held = attend(info, joined, sibling, start_row, 0, 5)
    if eight:
        both_near = after(both_near, held)
        up_near, out_own = both_near[..., : FF // 2], both_near[..., FF // 2 :]
        up_far = lax.ppermute(up_near, "seq", far_pairs)
    mixed, log_total = attend(info, joined, sibling, start_row, 5, 17, held)
    if eight:
        up_far = after(up_far, mixed)
        mixed = after(mixed, up_far, down_near)
        down_near = after(down_near, mixed)
        down_far = lax.ppermute(down_near, "seq", far_pairs)
        out_own = after(out_own, mixed)
        out_full, _ = whole(place, out_weight, [out_own] + from_sibling([out_own]))
    residual = x_float + dot_tn(out_full, mixed) + bias_out
    unit_two, inverse_two = norm_stats(residual)
    normed_two = (unit_two * gain_two + shift_two).astype(bf16)
    if eight:
        up_full = whole_of_quarters(place, up_weight, up_near, up_far, True)
    up_proj = dot_tn(up_full, normed_two) + bias_up
    active, slope_of = jax.vjp(lambda pre: jax.nn.gelu(pre, approximate=True), up_proj)
    slope = slope_of(jnp.ones_like(up_proj))[0].astype(bf16)
    active = active.astype(bf16)
    active, slope = lax.optimization_barrier((by_rows(active), by_rows(slope)))
    down_sum = GradSum(by_rows(dot_nt(active, cot).astype(bf16)), where, "rows")
    active = after(active, down_sum.operand)
    if eight:
        down_far = after(down_far, active)
        down_full = whole_of_quarters(place, down_weight, down_near, down_far)
    layer_cols = (residual + dot_tn(down_full, active) + bias_down).astype(bf16)

    down_sum.move(layer_cols)
    cot_two = after(cot, down_sum.operand)
    grad_up_proj = (dot_nn(down_full, cot_two) * slope.astype(f32)).astype(bf16)
    grad_up_proj = by_rows(grad_up_proj)
    grad_hidden = jnp.sum(grad_up_proj.astype(f32), axis=1)
    up_sum = GradSum(by_rows(dot_nt(normed_two, grad_up_proj).astype(bf16)), where, "columns")
    down_sum.move(up_sum.operand)
    grad_up_proj = after(grad_up_proj, up_sum.operand, down_sum.operand)
    grad_a2 = dot_nn(up_full, grad_up_proj)
    grad_gain_two = jnp.sum(grad_a2 * unit_two, axis=1)
    grad_shift_two = jnp.sum(grad_a2, axis=1)
    cot_float = cot.astype(f32)
    grad_residual = cot_float + norm_back(grad_a2, unit_two, inverse_two, gain_two)
    grad_branch = grad_residual.astype(bf16)

    up_sum.move(grad_branch)
    out_sum = GradSum(by_rows(dot_nt(mixed, grad_branch).astype(bf16)), where, "plain")
    grad_mixed = dot_nn(out_full, grad_branch).astype(bf16)
    out_sum.move(grad_mixed)
    grad_mixed = after(grad_mixed, up_sum.operand, out_sum.operand, down_sum.operand)
    back = functools.partial(
        attend_back, info, joined, sibling, start_row, mixed, grad_mixed, log_total
    )
    own_grads, sib_one = back(0, 6)
    own_grads = after(own_grads, sib_one)
    layer_out = give_back(after(layer_cols, sib_one), bf16, sib_one)
    own_grads, sib_two = back(6, 12, (own_grads,))
    sib_one = lax.ppermute(sib_one, "seq", sibling_pairs)
    up_sum.move(sib_two)
    out_sum.move()
    out_sum.move(sib_two)
    own_grads = after(own_grads, up_sum.operand, out_sum.operand)
    own_grads, sib_three = back(12, 17, (own_grads,))
    sib_two = lax.ppermute(sib_two, "seq", sibling_pairs)
    sib_three = lax.ppermute(sib_three, "seq", sibling_pairs)
    tokens_here = x_in.shape[1]
    from_sib = jnp.concatenate([sib_one, sib_two, sib_three], axis=1)
    key_value = (own_grads[1:].astype(f32) + from_sib.astype(f32)).astype(bf16)
    grad_joined = lax.dynamic_update_slice(own_grads, key_value, (1, 0, 0, 0))
    grad_joined = by_rows(grad_joined.reshape(3 * D, tokens_here))
    cut_at = 3 * D // 2
    first_sum = GradSum(
        by_rows(dot_nt(normed, grad_joined[:cut_at]).astype(bf16)), where, "hops"
    )
    grad_joined = after(grad_joined, first_sum.operand)
    joined_sums = jnp.sum(grad_joined.astype(f32), axis=1)
    first_sum.move(joined_sums)
    down_sum.move(joined_sums)
    grad_joined = after(grad_joined, first_sum.operand)
    grad_a1 = dot_nn(qkv_full, grad_joined)
    grad_gain_one = jnp.sum(grad_a1 * unit_one, axis=1)
    grad_shift_one = jnp.sum(grad_a1, axis=1)
    small_grads = jnp.stack(
        [
            grad_gain_one,
            grad_gain_two,
            grad_shift_one,
            grad_shift_two,
            joined_sums[:D],
            joined_sums[2 * D :],
            jnp.sum(grad_branch.astype(f32), axis=1),
            jnp.sum(cot_float, axis=1),
        ]
    )
    shards = lax.axis_size("dp")
    small_parts = jnp.concatenate(
        [
            jnp.transpose(small_grads.reshape(8, shards, shard), (1, 0, 2)),
            grad_hidden.reshape(shards, 4, shard),
        ],
        axis=1,
    )
    small_flat = small_parts.reshape(shards, 12 * shard)
    second_sum = GradSum(
        by_rows(dot_nt(normed, grad_joined[cut_at:]).astype(bf16)), where, "hops", small_flat
    )
    grad_x = grad_residual + norm_back(grad_a1, unit_one, inverse_one, gain_one)
    first_sum.move(second_sum.operand)
    second_sum.move(grad_x)
    up_sum.move(second_sum.operand)
    first_sum.move(second_sum.operand)
    second_sum.move(second_sum.operand)
    grad_tokens = give_back(grad_x, f32, second_sum.operand)
    layer_out = after(layer_out, second_sum.operand)
    for total in (first_sum, second_sum, down_sum, up_sum, out_sum):
        while total.stage < 5:
            total.move()
    grad_qkv = jnp.concatenate([first_sum.operand, second_sum.operand], axis=1)
    small_own = second_sum.extra.reshape(12, shard)
    hidden_own = small_own[8:].reshape(4 * shard)

    return (
        layer_out,
        grad_tokens,
        grad_qkv,
        out_sum.operand,
        up_sum.operand,
        down_sum.operand,
        small_own[0:2],
        small_own[2:4],
        small_own[4:8],
        hidden_own,
    )


def solution(mesh):
    placed = (
        P("dp", "seq", None),
        P("dp", None),
        P("dp", None),
        P("dp", None),
        P("dp", None),
        P(None, "dp"),
        P(None, "dp"),
        P(None, "dp"),
        P("dp"),
        P("dp", None),
        P("dp", "seq", None),
    )
    return jax.shard_map(
        body,
        mesh=mesh,
        in_specs=placed,
        out_specs=(
            P("dp", "seq", None),
            P("dp", "seq", None),
            P("dp", None),
            P("dp", None),
            P("dp", None),
            P("dp", None),
            P(None, "dp"),
            P(None, "dp"),
            P(None, "dp"),
            P("dp"),
        ),
        check_vma=False,
    )
```

```python
import functools

import jax
import jax.numpy as jnp
from jax import lax
from jax.experimental import pallas as pl
from jax.experimental.layout import Layout, with_layout_constraint
from jax.experimental.pallas import tpu as pltpu
from jax.sharding import PartitionSpec as P

D = 1088
H = 17
HD = 64
FF = 4352

norm_eps = 1e-05
masked_score = -1e30
score_scale = HD ** (-0.5)

TQ = 512
TK = 512
VMEM_BYTES = 56 * 1024 * 1024

f32 = jnp.float32
bf16 = jnp.bfloat16


def dot_tn(left, right):
    return lax.dot_general(left, right, (((0,), (0,)), ((), ())), preferred_element_type=f32)


def dot_nn(left, right):
    return lax.dot_general(left, right, (((1,), (0,)), ((), ())), preferred_element_type=f32)


def dot_nt(left, right):
    return lax.dot_general(left, right, (((1,), (1,)), ((), ())), preferred_element_type=f32)


def after(value, *others):
    return lax.optimization_barrier((value,) + others)[0]


def by_rows(value):
    return with_layout_constraint(value, Layout(major_to_minor=(0, 1)))


def norm_stats(rows):
    centre = rows - jnp.mean(rows, axis=0, keepdims=True)
    spread = jnp.mean(centre * centre, axis=0, keepdims=True)
    inverse = lax.rsqrt(spread + norm_eps)
    return centre * inverse, inverse


def norm_back(grad, unit, inverse, gain):
    scaled = grad * gain
    mean_one = jnp.mean(scaled, axis=0, keepdims=True)
    mean_two = jnp.mean(scaled * unit, axis=0, keepdims=True)
    return inverse * (scaled - mean_one - unit * mean_two)


def place_blocks(info_ref, store):
    for which in range(4):
        store(which // 2, which % 2, info_ref[which])


def allowed_mask(shape, key_first, query_first, start_row):
    key_pos = key_first + lax.broadcasted_iota(jnp.int32, shape, 0)
    query_pos = query_first + lax.broadcasted_iota(jnp.int32, shape, 1)
    return (key_pos <= query_pos) & (key_pos >= start_row)


def attend_kernel(
    info_ref, query_ref, key_ref, value_ref, key_sib_ref, value_sib_ref, start_ref,
    mixed_ref, log_ref, key_s, value_s,
):
    half = query_ref.shape[1] // 2
    ones_rows = jnp.ones((16, half), bf16)

    def store(sibling, part, block):
        key_from, value_from = (key_sib_ref, value_sib_ref) if sibling else (key_ref, value_ref)
        lanes = slice(part * half, (part + 1) * half)
        key_s[block] = key_from[:, lanes].astype(f32).T.astype(bf16)
        value_s[block] = jnp.concatenate([value_from[:, lanes], ones_rows], axis=0)

    place_blocks(info_ref, store)
    for part in range(2):
        lanes = slice(part * half, (part + 1) * half)
        query = query_ref[:, lanes] * jnp.asarray(score_scale, bf16)
        start_row = start_ref[:, lanes]
        own_block = info_ref[part]
        first = info_ref[4 + part]
        clear = info_ref[6 + part]

        def step(
            block, state, masked, keys=TK, queries=slice(0, TQ), query=query,
            start_row=start_row, own_block=own_block,
        ):
            peak, total = state
            scores = dot_nn(key_s[block, :keys], query[:, queries])
            if masked:
                allowed = allowed_mask(
                    scores.shape, block * TK, own_block * TQ + queries.start, start_row[:, queries]
                )
                scores = jnp.where(allowed, scores, masked_score)
            new_peak = jnp.maximum(peak, jnp.max(scores, axis=0, keepdims=True))
            weights = jnp.exp(scores - new_peak).astype(bf16)
            total = total * jnp.exp(peak - new_peak) + dot_nn(value_s[block, :, :keys], weights)
            return new_peak, total

        state = (
            jnp.full((1, half), masked_score, f32),
            jnp.zeros((HD + 16, half), f32),
        )
        state = lax.fori_loop(first, clear, functools.partial(step, masked=True), state)
        state = lax.fori_loop(clear, own_block, functools.partial(step, masked=False), state)
        for queries, keys in ((slice(0, TQ // 2), TK // 2), (slice(TQ // 2, TQ), TK)):
            peak, total = step(
                own_block, tuple(part[:, queries] for part in state), True, keys, queries
            )
            row_sum = total[HD : HD + 1]
            place = slice(lanes.start + queries.start, lanes.start + queries.stop)
            mixed_ref[:, place] = (total[:HD] / row_sum).astype(bf16)
            log_ref[0, :, place] = peak + jnp.log(row_sum)


def split_three(row):
    high = row.astype(bf16)
    rest = row - high.astype(f32)
    mid = rest.astype(bf16)
    low = (rest - mid.astype(f32)).astype(bf16)
    return high, mid, low


def with_rows(rows, row):
    high, mid, low = (part.astype(f32) for part in split_three(row))
    index = lax.broadcasted_iota(jnp.int32, (HD, row.shape[1]), 0)
    tail = jnp.where(index == 0, high, jnp.where(index == 1, mid, jnp.where(index == 2, low, 0.0)))
    return jnp.concatenate([rows, tail.astype(bf16)], axis=0)


def attend_back_kernel(
    info_ref, query_ref, key_ref, value_ref, key_sib_ref, value_sib_ref, start_ref,
    mixed_ref, grad_ref, log_ref,
    own_ref, sib_ref, key_s, value_s, key_t, grad_key_s, grad_value_s,
):
    half = query_ref.shape[1] // 2
    ones_cols = jnp.where(
        lax.broadcasted_iota(jnp.int32, (half, HD), 1) < 3, 1.0, 0.0
    ).astype(bf16)

    def store(sibling, part, block):
        key_from, value_from = (key_sib_ref, value_sib_ref) if sibling else (key_ref, value_ref)
        lanes = slice(part * half, (part + 1) * half)
        key_rows = key_from[:, lanes]
        key_t[block] = key_rows
        key_s[block] = jnp.concatenate([key_rows.astype(f32).T.astype(bf16), ones_cols], axis=1)
        value_s[block] = jnp.concatenate(
            [value_from[:, lanes].astype(f32).T.astype(bf16), ones_cols], axis=1
        )

    place_blocks(info_ref, store)
    grad_key_s[...] = jnp.zeros_like(grad_key_s)
    grad_value_s[...] = jnp.zeros_like(grad_value_s)
    for part in range(2):
        lanes = slice(part * half, (part + 1) * half)
        query = query_ref[:, lanes] * jnp.asarray(score_scale, bf16)
        grad = grad_ref[:, lanes]
        start_row = start_ref[:, lanes]
        delta = jnp.sum(
            grad.astype(f32) * mixed_ref[:, lanes].astype(f32), axis=0, keepdims=True
        )
        query_rows = with_rows(query, -log_ref[0, :, lanes])
        grad_rows = with_rows(grad, -delta)
        query_n = query.astype(f32).T.astype(bf16)
        grad_n = grad.astype(f32).T.astype(bf16)
        own_block = info_ref[part]
        first = info_ref[4 + part]
        clear = info_ref[6 + part]

        def step(
            block, grad_query, masked, keys=TK, queries=slice(0, TQ), query_rows=query_rows,
            grad_rows=grad_rows, query_n=query_n, grad_n=grad_n, start_row=start_row,
            own_block=own_block,
        ):
            weights = jnp.exp(dot_nn(key_s[block, :keys], query_rows[:, queries]))
            if masked:
                allowed = allowed_mask(
                    weights.shape, block * TK, own_block * TQ + queries.start, start_row[:, queries]
                )
                weights = jnp.where(allowed, weights, 0.0)
            grad_prob = dot_nn(value_s[block, :keys], grad_rows[:, queries])
            grad_score = (weights * grad_prob).astype(bf16)
            grad_value_s[block, :keys] += dot_nn(weights.astype(bf16), grad_n[queries])
            grad_key_s[block, :keys] += dot_nn(grad_score, query_n[queries])
            return grad_query + dot_nn(key_t[block, :, :keys], grad_score)

        grad_query = jnp.zeros((HD, half), f32)
        grad_query = lax.fori_loop(first, clear, functools.partial(step, masked=True), grad_query)
        grad_query = lax.fori_loop(
            clear, own_block, functools.partial(step, masked=False), grad_query
        )
        for queries, keys in ((slice(0, TQ // 2), TK // 2), (slice(TQ // 2, TQ), TK)):
            total = step(own_block, grad_query[:, queries], True, keys, queries)
            place = slice(lanes.start + queries.start, lanes.start + queries.stop)
            own_ref[0, 0, :, place] = (total * score_scale).astype(bf16)

    def give(sibling, part, block):
        lanes = slice(part * half, (part + 1) * half)
        key_rows = grad_key_s[block].T.astype(bf16)
        value_rows = grad_value_s[block].T.astype(bf16)
        if sibling:
            sib_ref[0, 0, :, lanes] = key_rows
            sib_ref[1, 0, :, lanes] = value_rows
        else:
            own_ref[1, 0, :, lanes] = key_rows
            own_ref[2, 0, :, lanes] = value_rows

    place_blocks(info_ref, give)


def head_spec(offset, tokens):
    return pl.BlockSpec((HD, tokens), lambda head, info: (head + offset, 0))


def attend(info, joined, sibling, start_row, first, last, held=()):
    tokens = joined.shape[1]
    blocks = 2 * tokens // TK
    heads = last - first

    def kernel(info_ref, *refs):
        attend_kernel(info_ref, *refs[:6], *refs[6 + len(held) :])

    return pl.pallas_call(
        kernel,
        out_shape=(
            jax.ShapeDtypeStruct((D, tokens), bf16),
            jax.ShapeDtypeStruct((H, 1, tokens), f32),
        ),
        grid_spec=pltpu.PrefetchScalarGridSpec(
            num_scalar_prefetch=1,
            grid=(heads,),
            in_specs=[
                head_spec(first, tokens),
                head_spec(H + first, tokens),
                head_spec(2 * H + first, tokens),
                head_spec(first, tokens),
                head_spec(H + first, tokens),
                pl.BlockSpec((1, tokens), lambda head, info: (0, 0)),
            ]
            + [pl.BlockSpec(memory_space=pl.ANY)] * len(held),
            out_specs=(
                head_spec(first, tokens),
                pl.BlockSpec((1, 1, tokens), lambda head, info: (head + first, 0, 0)),
            ),
            scratch_shapes=[
                pltpu.VMEM((blocks, TK, HD), bf16),
                pltpu.VMEM((blocks, HD + 16, TK), bf16),
            ],
        ),
        input_output_aliases={7 + i: i for i in range(len(held))},
        compiler_params=pltpu.CompilerParams(vmem_limit_bytes=VMEM_BYTES),
        cost_estimate=pl.CostEstimate(
            flops=10**6, bytes_accessed=10**5, transcendentals=0
        ),
        name="attend",
    )(info, joined, joined, joined, sibling, sibling, start_row, *held)


def attend_back(
    info, joined, sibling, start_row, mixed, grad_mixed, log_total, first, last, held=()
):
    tokens = joined.shape[1]
    blocks = 2 * tokens // TK
    heads = last - first

    def kernel(info_ref, *refs):
        attend_back_kernel(info_ref, *refs[:9], *refs[9 + len(held) :])

    return pl.pallas_call(
        kernel,
        out_shape=(
            jax.ShapeDtypeStruct((3, H, HD, tokens), bf16),
            jax.ShapeDtypeStruct((2, heads, HD, tokens), bf16),
        ),
        grid_spec=pltpu.PrefetchScalarGridSpec(
            num_scalar_prefetch=1,
            grid=(heads,),
            in_specs=[
                head_spec(first, tokens),
                head_spec(H + first, tokens),
                head_spec(2 * H + first, tokens),
                head_spec(first, tokens),
                head_spec(H + first, tokens),
                pl.BlockSpec((1, tokens), lambda head, info: (0, 0)),
                head_spec(first, tokens),
                head_spec(first, tokens),
                pl.BlockSpec((1, 1, tokens), lambda head, info: (head + first, 0, 0)),
            ]
            + [pl.BlockSpec(memory_space=pl.ANY)] * len(held),
            out_specs=(
                pl.BlockSpec((3, 1, HD, tokens), lambda head, info: (0, head + first, 0, 0)),
                pl.BlockSpec((2, 1, HD, tokens), lambda head, info: (0, head, 0, 0)),
            ),
            scratch_shapes=[
                pltpu.VMEM((blocks, TK, 2 * HD), bf16),
                pltpu.VMEM((blocks, TK, 2 * HD), bf16),
                pltpu.VMEM((blocks, HD, TK), bf16),
                pltpu.VMEM((blocks, TK, HD), f32),
                pltpu.VMEM((blocks, TK, HD), f32),
            ],
        ),
        input_output_aliases={10 + i: i for i in range(len(held))},
        compiler_params=pltpu.CompilerParams(vmem_limit_bytes=VMEM_BYTES),
        cost_estimate=pl.CostEstimate(
            flops=10**6, bytes_accessed=10**5, transcendentals=0
        ),
        name="attend_back",
    )(info, joined, joined, joined, sibling, sibling, start_row, mixed, grad_mixed, log_total, *held)


lines = [(i, (i + 2) % 8) for i in range(8)]
line_hops = [[(i, (i + 2 * hop) % 8) for i in range(8)] for hop in range(4)]
across = [(i, i ^ 1) for i in range(8)]
sibling_pairs = [(i, i ^ 1) for i in range(4)]
far_pairs = [(i, i ^ 2) for i in range(4)]
mirror_pairs = [(i, 3 - i) for i in range(4)]


def half_groups(groups):
    return (groups + 1) // 2


def assemble_kernel(info_ref, *refs, groups, half, pieces, by_columns):
    full_ref, extra_ref, stage, in_sems, out_sems = refs[-5:]
    z, x, core, far = info_ref[0], info_ref[1], info_ref[2], info_ref[3]
    slots, come, leave = list(range(8)), [], []
    for which in range(pieces):
        if pieces == 16:
            part = pl.ds((core if which < 8 else 1 - core) * half, half)
            hop, side = which % 4, (which // 4) % 2
            slot = lax.rem(z - hop + 4, 4) * 2 + (1 - x if side else x)
            if which < 8:
                slots[which] = slot
            target = stage.at[slot, part]
        else:
            side = core if which % 2 == 0 else 1 - core
            plane = far if which < 2 else 1 - far
            if pieces == 2:
                target = stage.at[:, pl.ds(side * half, half)]
            elif by_columns:
                width = stage.shape[3] // 2
                lanes = pl.ds(pl.multiple_of(plane * width, 128), width)
                target = stage.at[:, pl.ds(side * half, half), :, lanes]
            else:
                target = stage.at[:, pl.ds((plane * 2 + side) * half, half)]
        come.append(pltpu.make_async_copy(refs[which], target, in_sems.at[which]))
    for copy in come:
        copy.start()
    if pieces < 16:
        for copy in come:
            copy.wait()
    for index in range(8):
        slot = slots[index]
        if pieces == 16:
            come[index].wait()
            come[index + 8].wait()
        out = [
            pltpu.make_async_copy(
                stage.at[slot, pl.ds(0, groups)],
                full_ref.at[pl.ds(slot * groups, groups)],
                out_sems.at[index],
            )
        ]
        if pieces == 16:
            out.append(
                pltpu.make_async_copy(
                    stage.at[slot, pl.ds(groups, 1)],
                    extra_ref.at[pl.ds(slot, 1)],
                    out_sems.at[8 + index],
                )
            )
        for copy in out:
            copy.start()
        leave += out
    for copy in leave:
        copy.wait()


def assemble(info, pieces, groups, columns, by_columns=False):
    any_spec = pl.BlockSpec(memory_space=pl.ANY)
    half = pieces[0].shape[-3]
    staged = groups + groups % 2
    return pl.pallas_call(
        functools.partial(
            assemble_kernel, groups=groups, half=half, pieces=len(pieces), by_columns=by_columns
        ),
        out_shape=(
            jax.ShapeDtypeStruct((8 * groups, 8, columns), bf16),
            jax.ShapeDtypeStruct((8, 8, columns), bf16),
        ),
        grid_spec=pltpu.PrefetchScalarGridSpec(
            num_scalar_prefetch=1,
            grid=(1,),
            in_specs=[any_spec] * len(pieces),
            out_specs=(any_spec, any_spec),
            scratch_shapes=[
                pltpu.VMEM((8, staged, 8, columns), bf16),
                pltpu.SemaphoreType.DMA((len(pieces),)),
                pltpu.SemaphoreType.DMA((16,)),
            ],
        ),
        compiler_params=pltpu.CompilerParams(vmem_limit_bytes=VMEM_BYTES),
        cost_estimate=pl.CostEstimate(
            flops=0, bytes_accessed=10**5, transcendentals=0
        ),
        name="assemble",
    )(info, *pieces)


def core_piece(weight, core, extra=None):
    rows, columns = weight.shape
    groups = rows // 8
    half = half_groups(groups)
    grouped = weight.reshape(groups, 8, columns)
    if 2 * half > groups:
        spare = jnp.zeros((1, 8, columns), weight.dtype)
        if extra is not None:
            spare = lax.dynamic_update_slice(spare, extra.reshape(1, 1, -1), (0, 0, 0))
        grouped = jnp.concatenate([grouped, spare], axis=0)
    return lax.dynamic_slice_in_dim(grouped, core * half, half, 0)


def along_line(piece):
    line = [piece]
    for _ in range(3):
        line.append(lax.ppermute(line[-1], "dp", lines))
    return line


def from_all(piece):
    groups, _, columns = piece.shape
    flat = lax.all_gather(piece.reshape(groups * 8, columns), "dp", axis=0, tiled=True)
    return flat.reshape(8, groups, 8, columns)


def from_across(parts):
    return [lax.ppermute(part, "dp", across) for part in parts]


def from_sibling(parts):
    return [lax.ppermute(part, "seq", sibling_pairs) for part in parts]


def whole(info, weight, pieces, by_columns=False):
    rows, columns = weight.shape
    full, spare = assemble(info, pieces, rows // 8, columns, by_columns)
    return full.reshape(8 * rows, columns), spare


def whole_of_quarters(info, weight, near, far, by_columns=False):
    near_sib, far_sib = from_sibling([near, far])
    return whole(info, weight, [near, near_sib, far, far_sib], by_columns)[0]


class GradSum:
    def __init__(self, grad, place, kind):
        self.z, self.x, self.core, self.plane = place
        self.shards = lax.axis_size("dp")
        self.rows = grad.shape[0] // self.shards
        self.columns = grad.shape[1]
        self.kind = kind
        grad = grad.astype(bf16)
        self.stage = 0
        self.operand = grad
        if self.shards == 8:
            groups = self.rows // 8
            parts = grad.reshape(8, groups, 8, self.columns)
            if kind == "rows":
                self.half = self.even = groups // 4
                parts = parts.reshape(8, 2, groups // 2, 8, self.columns)
            else:
                self.half = half_groups(groups)
                self.even = groups - self.half
            if kind == "hops":
                parts = parts.reshape((4, 2) + parts.shape[1:])
            self.parts = parts
            self.operand = self.core_part(1 - self.core)

    def core_part(self, which):
        axis = self.parts.ndim - 3
        return lax.dynamic_slice_in_dim(self.parts, which * self.even, self.half, axis)

    def chunk(self, which):
        mine = lax.dynamic_index_in_dim(self.keep, which, 0, keepdims=False)
        theirs = lax.dynamic_index_in_dim(self.came, which, 0, keepdims=False)
        return mine.astype(f32) + theirs.astype(f32)

    def plane_part(self, value, which):
        if self.kind == "rows":
            return lax.dynamic_index_in_dim(value, which, 1, keepdims=False)
        width = self.columns // 2
        return lax.dynamic_slice_in_dim(value, which * width, width, 3)

    def move(self, *beside):
        self.stage += 1
        if self.shards != 8:
            if self.stage == 5:
                part = lax.psum_scatter(self.operand, "dp", scatter_dimension=0, tiled=True)
                self.operand = lax.psum(part, "seq").astype(f32)
            return
        core, x, z, plane = self.core, self.x, self.z, self.plane
        hops = self.kind == "hops"

        def arrived(value):
            return after(value, *beside) if beside else value

        if self.stage == 1:
            from_core = arrived(lax.ppermute(self.operand, "seq", sibling_pairs))
            chip = self.core_part(core).astype(f32) + from_core.astype(f32)
            if hops:
                self.operand = lax.dynamic_index_in_dim(chip, 1 - x, 1, keepdims=False).astype(bf16)
                self.keep = lax.dynamic_index_in_dim(chip, x, 1, keepdims=False).astype(bf16)
            elif self.kind == "plain":
                self.operand = chip.astype(bf16)
            else:
                self.operand = self.plane_part(chip, 1 - plane).astype(bf16)
                self.keep = self.plane_part(chip, plane).astype(bf16)
        elif self.stage == 2:
            if hops:
                self.came = arrived(lax.ppermute(self.operand, "dp", across))
                self.operand = [
                    self.chunk(lax.rem(z + hop, 4)).astype(bf16) for hop in range(1, 4)
                ]
            elif self.kind != "plain":
                came = arrived(lax.ppermute(self.operand, "seq", far_pairs))
                self.operand = (self.keep.astype(f32) + came.astype(f32)).astype(bf16)
        elif self.stage == 3:
            if hops:
                moved = arrived(
                    [
                        lax.ppermute(self.operand[hop - 1], "dp", line_hops[hop])
                        for hop in range(1, 4)
                    ]
                )
                total = self.chunk(z)
                for part in moved:
                    total = total + part.astype(f32)
                self.operand = total.astype(bf16)
            else:
                columns = self.operand.shape[-1]
                flat = self.operand.reshape(-1, columns)
                self.operand = arrived(
                    lax.psum_scatter(flat, "dp", scatter_dimension=0, tiled=True)
                )
        elif self.stage == 4:
            far = arrived(lax.ppermute(self.operand, "seq", far_pairs))
            if hops or self.kind == "plain":
                self.operand = (self.operand.astype(f32) + far.astype(f32)).astype(bf16)
            else:
                first = jnp.where(plane == 0, self.operand, far)
                second = jnp.where(plane == 0, far, self.operand)
                axis = 1 if self.kind == "columns" else 0
                self.operand = jnp.stack([first, second]) if axis == 0 else jnp.concatenate([first, second], axis=1)
        else:
            own = self.operand
            sib = arrived(lax.ppermute(own, "seq", sibling_pairs))
            if self.kind == "rows":
                first = jnp.where(core == 0, own, sib)
                second = jnp.where(core == 0, sib, own)
                both = jnp.stack([first, second], axis=1)
                self.operand = both.reshape(self.rows, self.columns).astype(f32)
            else:
                own = own.reshape(self.half * 8, self.columns)
                sib = sib.reshape(self.half * 8, self.columns)
                first = jnp.where(core == 0, own, sib)
                second = jnp.where(core == 0, sib, own)
                cut = (self.half - self.even) * 8
                both = jnp.concatenate([first, second[cut:]], axis=0).astype(f32)
                self.operand = both


def body(
    tokens,
    qkv_weight,
    out_weight,
    up_weight,
    down_weight,
    norm_gain,
    norm_shift,
    bias_rows,
    bias_hidden,
    doc_lengths,
    cotangent,
):
    block_rows = tokens.shape[1]
    length = block_rows * lax.axis_size("seq")
    shard = tokens.shape[2] // lax.axis_size("dp")
    own = lax.axis_index("seq")
    dp_index = lax.axis_index("dp")
    core = own % 2
    kept = own // 2
    z, x = dp_index // 2, dp_index % 2
    place = jnp.stack([z, x, core, kept]).astype(jnp.int32)
    where = (z, x, core, kept)

    small = jnp.concatenate(
        [norm_gain, norm_shift, bias_rows, bias_hidden.reshape(4, shard)], axis=0
    )
    eight = lax.axis_size("dp") == 8
    if eight:
        qkv_line = along_line(core_piece(qkv_weight, core, small))
        qkv_own = qkv_line + from_across(qkv_line)
        qkv_full, spare = whole(place, qkv_weight, qkv_own + from_sibling(qkv_own))
        small_all = spare[:, 0, : small.size].reshape(8, 12, shard).astype(f32)
        up_part = lax.dynamic_slice_in_dim(core_piece(up_weight, core), kept * (FF // 2), FF // 2, 2)
        both_part = jnp.concatenate([up_part, core_piece(out_weight, core)], axis=2)
        both_near = from_all(after(both_part, qkv_line[2]))
        quarter = down_weight.shape[0] // 4
        down_part = lax.dynamic_slice_in_dim(down_weight, own * quarter, quarter, 0)
        down_near = from_all(after(down_part.reshape(-1, 8, D), qkv_own[5]))
    else:
        small_all = lax.all_gather(small, "dp", axis=0).astype(f32)
        qkv_full, out_full, up_full, down_full = (
            lax.all_gather(weight, "dp", axis=0, tiled=True)
            for weight in (qkv_weight, out_weight, up_weight, down_weight)
        )
    small_rows = jnp.transpose(small_all[:, :8], (1, 0, 2)).reshape(8, D)
    small_cols = small_rows.T
    gain_one, gain_two = small_cols[:, 0:1], small_cols[:, 1:2]
    shift_one, shift_two = small_cols[:, 2:3], small_cols[:, 3:4]
    bias_query, bias_value = small_cols[:, 4:5], small_cols[:, 5:6]
    bias_out, bias_down = small_cols[:, 6:7], small_cols[:, 7:8]
    bias_up = small_all[:, 8:].reshape(FF, 1)

    def take(rows):
        cols = jnp.transpose(rows, (0, 2, 1))
        keep = lax.dynamic_index_in_dim(cols, kept, 0, keepdims=False)
        give = lax.dynamic_index_in_dim(cols, 1 - kept, 0, keepdims=False)
        return jnp.concatenate([keep, lax.ppermute(give, "seq", mirror_pairs)], axis=1)

    def mirrored(cols):
        return lax.ppermute(cols[:, block_rows:].astype(bf16), "seq", mirror_pairs)

    def give_back(cols, got, dtype):
        keep = cols[:, :block_rows]
        keep, got = keep.astype(dtype), got.astype(dtype)
        first = jnp.where(kept == 0, keep, got)
        second = jnp.where(kept == 0, got, keep)
        return jnp.transpose(jnp.stack([first, second]), (0, 2, 1))

    x_in = take(tokens)
    cot = take(cotangent)

    lengths = lax.dynamic_index_in_dim(doc_lengths, kept, 0, keepdims=False)
    bounds = jnp.cumsum(lengths)[:-1].astype(jnp.int32)
    mirror = 3 - own
    inside = jnp.arange(block_rows, dtype=jnp.int32)
    positions = jnp.concatenate([own * block_rows + inside, mirror * block_rows + inside])
    starts = jnp.max(jnp.where(bounds[:, None] <= positions[None, :], bounds[:, None], 0), axis=0)
    firsts = jnp.stack([starts[0], starts[block_rows]]) // TK
    lasts = jnp.stack([starts[block_rows - 1], starts[2 * block_rows - 1]])
    own_blocks = jnp.stack([own, mirror])
    clears = jnp.minimum((lasts + TK - 1) // TK, own_blocks)
    near = own ^ 1
    info = jnp.concatenate(
        [own_blocks, jnp.stack([near, 3 - near]), jnp.minimum(firsts, clears), clears]
    ).astype(jnp.int32)
    start_row = starts[None, :]

    x_float = x_in.astype(f32)
    unit_one, inverse_one = norm_stats(x_float)
    normed = (unit_one * gain_one + shift_one).astype(bf16)
    joined_bias = jnp.concatenate([bias_query, jnp.zeros_like(bias_query), bias_value], axis=0)
    joined = (dot_tn(qkv_full, normed) + joined_bias).astype(bf16)
    sibling = lax.ppermute(joined[D:], "seq", sibling_pairs)
    held = attend(info, joined, sibling, start_row, 0, 5)
    if eight:
        both_near = after(both_near, held)
        up_near, out_own = both_near[..., : FF // 2], both_near[..., FF // 2 :]
        up_far = lax.ppermute(up_near, "seq", far_pairs)
    mixed, log_total = attend(info, joined, sibling, start_row, 5, 17, held)
    if eight:
        up_far = after(up_far, mixed)
        mixed = after(mixed, up_far, down_near)
        down_near = after(down_near, mixed)
        down_far = lax.ppermute(down_near, "seq", far_pairs)
        out_own = after(out_own, mixed)
        out_full, _ = whole(place, out_weight, [out_own] + from_sibling([out_own]))
    residual = x_float + dot_tn(out_full, mixed) + bias_out
    unit_two, inverse_two = norm_stats(residual)
    normed_two = (unit_two * gain_two + shift_two).astype(bf16)
    if eight:
        up_full = whole_of_quarters(place, up_weight, up_near, up_far, True)
    up_proj = dot_tn(up_full, normed_two) + bias_up
    active, slope_of = jax.vjp(lambda pre: jax.nn.gelu(pre, approximate=True), up_proj)
    slope = slope_of(jnp.ones_like(up_proj))[0].astype(bf16)
    active = active.astype(bf16)
    active, slope = lax.optimization_barrier((by_rows(active), by_rows(slope)))
    down_sum = GradSum(by_rows(dot_nt(active, cot).astype(bf16)), where, "rows")
    active = after(active, down_sum.operand)
    if eight:
        down_far = after(down_far, active)
        down_full = whole_of_quarters(place, down_weight, down_near, down_far)
    layer_cols = (residual + dot_tn(down_full, active) + bias_down).astype(bf16)

    down_sum.move(layer_cols)
    cot_two = after(cot, down_sum.operand)
    grad_up_proj = (dot_nn(down_full, cot_two) * slope.astype(f32)).astype(bf16)
    grad_up_proj = by_rows(grad_up_proj)
    grad_hidden = jnp.sum(grad_up_proj.astype(f32), axis=1)
    up_sum = GradSum(by_rows(dot_nt(normed_two, grad_up_proj).astype(bf16)), where, "columns")
    down_sum.move(up_sum.operand)
    grad_up_proj = after(grad_up_proj, up_sum.operand, down_sum.operand)
    grad_a2 = dot_nn(up_full, grad_up_proj)
    grad_gain_two = jnp.sum(grad_a2 * unit_two, axis=1)
    grad_shift_two = jnp.sum(grad_a2, axis=1)
    cot_float = cot.astype(f32)
    grad_residual = cot_float + norm_back(grad_a2, unit_two, inverse_two, gain_two)
    grad_branch = grad_residual.astype(bf16)

    up_sum.move(grad_branch)
    out_sum = GradSum(by_rows(dot_nt(mixed, grad_branch).astype(bf16)), where, "hops")
    grad_mixed = dot_nn(out_full, grad_branch).astype(bf16)
    out_sum.move(grad_mixed)
    grad_mixed = after(grad_mixed, out_sum.operand, up_sum.operand)
    back = functools.partial(
        attend_back, info, joined, sibling, start_row, mixed, grad_mixed, log_total
    )
    own_grads, sib_one = back(0, 8)
    up_sum.move(sib_one)
    out_sum.move(sib_one)
    own_grads = after(own_grads, sib_one, up_sum.operand, out_sum.operand)
    own_grads, sib_two = back(8, 13, (own_grads,))
    sib_one = lax.ppermute(sib_one, "seq", sibling_pairs)
    got = after(mirrored(after(layer_cols, up_sum.operand)), sib_two)
    layer_out = give_back(layer_cols, got, bf16)
    down_sum.move(sib_two)
    out_sum.move(sib_two)
    own_grads = after(own_grads, sib_two, down_sum.operand, layer_out, out_sum.operand)
    own_grads, sib_three = back(13, 17, (own_grads,))
    sib_two = lax.ppermute(sib_two, "seq", sibling_pairs)
    sib_three = lax.ppermute(sib_three, "seq", sibling_pairs)
    up_sum.move(sib_three)
    down_sum.move(sib_three)
    out_sum.move(sib_three)
    tokens_here = x_in.shape[1]
    from_sib = jnp.concatenate([sib_one, sib_two, sib_three], axis=1)
    key_value = (own_grads[1:].astype(f32) + from_sib.astype(f32)).astype(bf16)
    grad_joined = lax.dynamic_update_slice(own_grads, key_value, (1, 0, 0, 0))
    grad_joined = by_rows(grad_joined.reshape(3 * D, tokens_here))
    cut_at = 3 * D // 2
    first_sum = GradSum(
        by_rows(dot_nt(normed, grad_joined[:cut_at]).astype(bf16)), where, "hops"
    )
    grad_joined = after(grad_joined, first_sum.operand)
    second_sum = GradSum(
        by_rows(dot_nt(normed, grad_joined[cut_at:]).astype(bf16)), where, "hops"
    )
    first_sum.move(second_sum.operand)
    joined_sums = jnp.sum(after(grad_joined, first_sum.operand).astype(f32), axis=1)
    second_sum.move(joined_sums)
    grad_joined = after(grad_joined, second_sum.operand, joined_sums)
    grad_a1 = dot_nn(qkv_full, grad_joined)
    grad_gain_one = jnp.sum(grad_a1 * unit_one, axis=1)
    grad_shift_one = jnp.sum(grad_a1, axis=1)

    small_grads = jnp.stack(
        [
            grad_gain_one,
            grad_gain_two,
            grad_shift_one,
            grad_shift_two,
            joined_sums[:D],
            joined_sums[2 * D :],
            jnp.sum(grad_branch.astype(f32), axis=1),
            jnp.sum(cot_float, axis=1),
        ]
    )
    shards = lax.axis_size("dp")
    small_parts = jnp.concatenate(
        [
            jnp.transpose(small_grads.reshape(8, shards, shard), (1, 0, 2)),
            grad_hidden.reshape(shards, 4, shard),
        ],
        axis=1,
    )
    small_flat = jnp.pad(small_parts.reshape(shards, 1, 12 * shard), ((0, 0), (0, 7), (0, 0)))
    small_sum = GradSum(small_flat.reshape(shards * 8, 12 * shard), where, "hops")
    grad_x = grad_residual + norm_back(grad_a1, unit_one, inverse_one, gain_one)
    first_sum.move(grad_x)
    first_operand = first_sum.operand
    got = mirrored(grad_x)
    small_sum.move(first_operand)
    second_sum.move(first_operand)
    small_sum.operand = after(small_sum.operand, second_sum.operand)
    up_sum.operand = after(up_sum.operand, second_sum.operand)
    first_sum.move(second_sum.operand)
    second_sum.move()
    up_sum.move(second_sum.operand)
    grad_tokens = give_back(grad_x, after(got, second_sum.operand), f32)
    for total in (first_sum, second_sum, small_sum, up_sum, down_sum, out_sum):
        while total.stage < 5:
            total.move()
    grad_qkv = jnp.concatenate([first_sum.operand, second_sum.operand], axis=1)
    small_own = small_sum.operand[0].reshape(12, shard)
    hidden_own = small_own[8:].reshape(4 * shard)

    return (
        layer_out,
        grad_tokens,
        grad_qkv,
        out_sum.operand,
        up_sum.operand,
        down_sum.operand,
        small_own[0:2],
        small_own[2:4],
        small_own[4:8],
        hidden_own,
    )


def solution(mesh):
    placed = (
        P("dp", "seq", None),
        P("dp", None),
        P("dp", None),
        P("dp", None),
        P("dp", None),
        P(None, "dp"),
        P(None, "dp"),
        P(None, "dp"),
        P("dp"),
        P("dp", None),
        P("dp", "seq", None),
    )
    return jax.shard_map(
        body,
        mesh=mesh,
        in_specs=placed,
        out_specs=(
            P("dp", "seq", None),
            P("dp", "seq", None),
            P("dp", None),
            P("dp", None),
            P("dp", None),
            P("dp", None),
            P(None, "dp"),
            P(None, "dp"),
            P(None, "dp"),
            P("dp"),
        ),
        check_vma=False,
    )
```
